32 devices in a mesh: rep: 4 (over z), shard: 4 (over x, core), tp: 2 (over y).
Axes of the slice: x: 2, y: 2, z: 4, core: 2. Of those that a mesh axis runs over, the one named last changes fastest.
Arguments:
- delta_inputs: bfloat16 [4, 2, 768, 2304], P('rep', None, 'shard', 'tp'), may hold values from -6 to 6
- delta_mixing: bfloat16 [4, 2, 768, 768], P('rep', None, 'shard', 'tp'), may hold values from -6 to 6
- delta_expand: bfloat16 [4, 2, 768, 3072], P('rep', None, 'shard', 'tp'), may hold values from -6 to 6
- delta_reduce: bfloat16 [4, 2, 3072, 768], P('rep', None, 'shard', 'tp'), may hold values from -6 to 6
- owner_weights: float32 [4, 4, 2, 442368], P('rep', 'shard', 'tp'), may hold values from -6 to 6
- owner_momentum: float32 [4, 4, 2, 442368], P('rep', 'shard', 'tp'), may hold values from -6 to 6
- delta_embed: bfloat16 [4, 50304, 768], P('rep', 'shard', 'tp'), may hold values from -6 to 6
- embed_owner: float32 [4, 4, 3144, 768], P('shard', 'rep', None, 'tp'), may hold values from -6 to 6
- embed_momentum: float32 [4, 4, 3144, 64], P('shard', 'rep'), may hold values from -6 to 6
- basis: float32 [768, 64], P('tp'), may hold values from -0.21875 to 0.21875
Outputs:
- fresh_inputs: bfloat16 [2, 768, 2304], P(None, 'shard', 'tp')
- fresh_mixing: bfloat16 [2, 768, 768], P(None, 'shard', 'tp')
- fresh_expand: bfloat16 [2, 768, 3072], P(None, 'shard', 'tp')
- fresh_reduce: bfloat16 [2, 3072, 768], P(None, 'shard', 'tp')
- next_weights: float32 [4, 4, 2, 442368], P('rep', 'shard', 'tp')
- next_momentum: float32 [4, 4, 2, 442368], P('rep', 'shard', 'tp')
- fresh_embed: bfloat16 [50304, 768], P('shard', 'tp')
- next_embed: float32 [4, 4, 3144, 768], P('shard', 'rep', None, 'tp')
- next_embed_momentum: float32 [4, 4, 3144, 64], P('shard', 'rep')
The draws below stay inside these ranges and needn't reach their ends.
All inputs are finite; a program needn't handle non-finite values.
Results may differ from the reference program's by a relative error of at most 0.0085.
Values may be sent and summed in bfloat16 or wider, within the bound.
No kernel may reach another device: no remote copies, remote signals or barrier semaphores. Data moves between devices by JAX's collectives and lax.ppermute only.
A program may use at most 128 MiB of HBM per device.

```python
import jax
import jax.numpy as jnp
from jax import lax

D = 768
FF = 3072
VOCAB = 50304
RANK = 64
LAYERS = 2
FLAT = 442368
N_REP = 4
N_SHARD = 4
N_TP = 2


def block_levels(rng, shape, cuts, low, top_value):
    level, own = 1.0, jax.random.fold_in(rng, 6)
    for dim, shards_of in cuts:
        steps = jnp.exp(jax.random.uniform(jax.random.fold_in(own, dim), (shards_of,), jnp.float32, low / len(cuts), top_value / len(cuts)))
        level = level * jnp.repeat(steps, shape[dim] // shards_of).reshape([-1 if axis == dim else 1 for axis in range(len(shape))])
    return level


def normal_values(stream_key, dims, spread, most, shards=(), kind=jnp.bfloat16):
    drawn = spread * jax.random.normal(stream_key, dims, jnp.float32)
    if shards:
        drawn = drawn * block_levels(stream_key, dims, shards, -0.22, 0.18)
    return jnp.clip(drawn, -most, most).astype(kind)


def setup_inputs(seed: int = 0) -> dict:
    splits = jax.random.split(jax.random.key(seed), 11)
    delta_inputs = normal_values(splits[0], (N_REP, LAYERS, D, 3 * D), 1.0, 6.0, ((0, 4), (2, 4), (3, 2)))
    delta_mixing = normal_values(splits[1], (N_REP, LAYERS, D, D), 1.0, 6.0, ((0, 4), (2, 4), (3, 2)))
    delta_expand = normal_values(splits[2], (N_REP, LAYERS, D, FF), 1.0, 6.0, ((0, 4), (2, 4), (3, 2)))
    delta_reduce = normal_values(splits[3], (N_REP, LAYERS, FF, D), 1.0, 6.0, ((0, 4), (2, 4), (3, 2)))
    owner_weights = normal_values(splits[4], (N_REP, N_SHARD, N_TP, FLAT), 1.0, 6.0, ((0, 4), (1, 4), (2, 2)), jnp.float32)
    owner_momentum = normal_values(splits[5], (N_REP, N_SHARD, N_TP, FLAT), 1.0, 6.0, ((0, 4), (1, 4), (2, 2)), jnp.float32)
    delta_embed = normal_values(splits[6], (N_REP, VOCAB, D), 1.0, 6.0, ((0, 4), (1, 4), (2, 2)))
    embed_owner = normal_values(splits[7], (N_SHARD, N_REP, VOCAB // (N_SHARD * N_REP), D), 1.0, 6.0, ((0, 4), (1, 4), (3, 2)), jnp.float32)
    embed_momentum = normal_values(splits[8], (N_SHARD, N_REP, VOCAB // (N_SHARD * N_REP), RANK), 1.0, 6.0, ((0, 4), (1, 4)), jnp.float32)
    basis = normal_values(splits[9], (D, RANK), D ** -0.5, 0.21875, ((0, 2),), jnp.float32)
    return {"delta_inputs": delta_inputs, "delta_mixing": delta_mixing, "delta_expand": delta_expand, "delta_reduce": delta_reduce, "owner_weights": owner_weights, "owner_momentum": owner_momentum, "delta_embed": delta_embed, "embed_owner": embed_owner, "embed_momentum": embed_momentum, "basis": basis}


MOMENTUM = 0.5
OUTER_RATE = 0.7


def to_owner(array, rows, cols):
    sub = rows // (N_SHARD * N_REP)
    piece = cols // (N_TP * N_SHARD)
    view = array.reshape(LAYERS, N_SHARD, N_REP, sub, N_TP, N_SHARD, piece)
    view = jnp.transpose(view, (2, 5, 4, 0, 3, 1, 6))
    return view.reshape(N_REP, N_SHARD, N_TP, LAYERS * sub * N_SHARD * piece)


def from_owner(flat_part, rows, cols):
    sub = rows // (N_SHARD * N_REP)
    piece = cols // (N_TP * N_SHARD)
    view = flat_part.reshape(N_REP, N_SHARD, N_TP, LAYERS, sub, N_SHARD, piece)
    view = jnp.transpose(view, (3, 5, 0, 4, 2, 1, 6))
    return view.reshape(LAYERS, rows, cols)


def reference(delta_inputs, delta_mixing, delta_expand, delta_reduce, owner_weights, owner_momentum, delta_embed, embed_owner, embed_momentum, basis):
    deltas = (delta_inputs, delta_mixing, delta_expand, delta_reduce)
    shapes = ((D, 3 * D), (D, D), (D, FF), (FF, D))
    pieces = []
    for delta, shape in zip(deltas, shapes):
        mean_value = jnp.sum(delta, axis=0, dtype=jnp.float32) / N_REP
        pieces.append(to_owner(mean_value, shape[0], shape[1]))
    gradient = jnp.concatenate(pieces, axis=3)
    next_momentum = MOMENTUM * owner_momentum + gradient
    next_weights = owner_weights - OUTER_RATE * (gradient + MOMENTUM * next_momentum)
    copies = next_weights.astype(jnp.bfloat16)
    fresh = []
    offset = 0
    for shape in shapes:
        count = LAYERS * shape[0] * shape[1] // (N_REP * N_SHARD * N_TP)
        fresh.append(from_owner(copies[..., offset:offset + count], shape[0], shape[1]))
        offset = offset + count
    embed_mean = jnp.sum(delta_embed, axis=0, dtype=jnp.float32) / N_REP
    coefficients = jnp.dot(embed_mean, basis, precision=lax.Precision.HIGHEST, preferred_element_type=jnp.float32)
    momentum_rows = MOMENTUM * embed_momentum.reshape(VOCAB, RANK) + coefficients
    direction = coefficients + MOMENTUM * momentum_rows
    table = embed_owner.reshape(VOCAB, D) - OUTER_RATE * jnp.dot(direction, basis.T, precision=lax.Precision.HIGHEST, preferred_element_type=jnp.float32)
    fresh_embed = table.astype(jnp.bfloat16)
    next_embed = table.reshape(embed_owner.shape)
    next_embed_momentum = momentum_rows.reshape(embed_momentum.shape)
    return (fresh[0], fresh[1], fresh[2], fresh[3], next_weights, next_momentum, fresh_embed, next_embed, next_embed_momentum)
```

```python
import jax
import jax.numpy as jnp
from jax import lax
from jax.sharding import PartitionSpec as P

MOMENTUM = 0.5
OUTER_RATE = 0.7

OUT_IN = [(0, 1), (3, 2)]
MIDDLE = [(1, 2), (2, 1)]
IN_OUT = [(1, 0), (2, 3)]


def permute(value, pairs):
    return lax.ppermute(value, "rep", pairs)


def block_of(place):
    rank = lax.axis_index("rep")
    return jnp.where(rank >= 2, 3 - place, place)


def line_sum(own):
    wide = lambda value: value.astype(jnp.float32)
    add = lambda one, two: (wide(one) + wide(two)).astype(one.dtype)
    far, middle, near, last = (own(block_of(place)) for place in (3, 2, 1, 0))
    far_in = permute(far, OUT_IN)
    middle_in = permute(middle, OUT_IN)
    near_in = permute(near, OUT_IN)
    far_across = permute(add(far, far_in), MIDDLE)
    middle_across = permute(add(middle, middle_in), MIDDLE)
    last_out = permute(add(last, far_across), IN_OUT)
    rank = lax.axis_index("rep")
    mine = jnp.where((rank == 0) | (rank == 3), last, near)
    return wide(mine) + wide(near_in) + wide(middle_across) + wide(last_out)


def line_gather(mine):
    rank = lax.axis_index("rep")
    end = (rank == 0) | (rank == 3)
    to_end = permute(mine, IN_OUT)
    across = permute(mine, MIDDLE)
    to_inner = permute(mine, OUT_IN)
    to_end_2 = permute(across, IN_OUT)
    across_2 = permute(to_inner, MIDDLE)
    to_end_3 = permute(across_2, IN_OUT)
    return [
        (rank, mine),
        (block_of(jnp.where(end, 1, 0)), jnp.where(end, to_end, to_inner)),
        (block_of(2), jnp.where(end, to_end_2, across)),
        (block_of(3), jnp.where(end, to_end_3, across_2)),
    ]


def local(
    delta_inputs,
    delta_mixing,
    delta_expand,
    delta_reduce,
    owner_weights,
    owner_momentum,
    delta_embed,
    embed_owner,
    embed_momentum,
    basis,
):
    groups = lax.axis_size("rep")
    shards = lax.axis_size("shard")
    deltas = (delta_inputs, delta_mixing, delta_expand, delta_reduce)
    layers = delta_inputs.shape[1]
    width = min(delta.shape[3] for delta in deltas)
    sub = min(delta.shape[2] for delta in deltas) // groups

    rows = embed_owner.shape[2]
    half_rank = basis.shape[1] // 2
    sent_rows = embed_owner[0, 0].astype(jnp.bfloat16)
    all_rows = lax.all_gather(sent_rows, "rep", axis=0, tiled=False)

    terms = lax.dot_general(
        basis,
        delta_embed[0].astype(jnp.float32),
        (((0,), (1,)), ((), ())),
        precision=lax.Precision.HIGH,
        preferred_element_type=jnp.float32,
    ).astype(jnp.bfloat16)
    side = lax.axis_index("tp")
    keep = lax.dynamic_slice_in_dim(terms, side * half_rank, half_rank, 0)
    give = lax.dynamic_slice_in_dim(terms, (1 - side) * half_rank, half_rank, 0)
    swap = [(0, 1), (1, 0)]
    taken = lax.ppermute(give, "tp", swap)
    kept = (keep.astype(jnp.float32) + taken.astype(jnp.float32)).astype(jnp.bfloat16)

    def dense_block(block):
        panels = []
        for delta in deltas:
            count = delta.shape[2] // groups
            part = lax.dynamic_slice_in_dim(delta[0], block * count, count, 1)
            part = part.reshape(layers, count // sub, sub, part.shape[2] // width, width)
            part = part.transpose(1, 3, 0, 2, 4)
            panels.append(part.reshape(-1, layers, sub, width))
        return jnp.concatenate(panels)

    def pieces(block):
        parts = []
        at = 0
        for delta in deltas:
            over = delta.shape[2] // groups // sub
            across = delta.shape[3] // width
            part = block[at : at + over * across].reshape(over, across, layers, sub, width)
            part = part.transpose(2, 0, 3, 1, 4).reshape(layers, over, sub, across * width)
            parts.append(part)
            at = at + over * across
        return parts

    summed = line_sum(dense_block).astype(jnp.bfloat16)
    sending = []
    for part in pieces(summed):
        over, cols = part.shape[1], part.shape[3]
        part = part.reshape(layers, over, sub, shards, cols // shards).transpose(3, 0, 2, 1, 4)
        sending.append(part.reshape(shards, layers, sub, over * cols // shards))
    moved = lax.all_to_all(jnp.concatenate(sending, axis=3), "shard", split_axis=0, concat_axis=0, tiled=True)
    at = 0
    flats = []
    for delta in deltas:
        over = delta.shape[2] // groups // sub
        piece = delta.shape[3] // shards
        part = moved[..., at : at + over * piece].reshape(shards, layers, sub, over, piece)
        flats.append(part.transpose(1, 3, 2, 0, 4).reshape(-1))
        at = at + over * piece
    gradient = (jnp.concatenate(flats).astype(jnp.float32) / groups).reshape(owner_weights.shape)
    next_momentum = MOMENTUM * owner_momentum + gradient
    next_weights = owner_weights - OUTER_RATE * (gradient + MOMENTUM * next_momentum)
    copies = next_weights.astype(jnp.bfloat16).reshape(-1)
    returning = []
    offset = 0
    for delta in deltas:
        over = delta.shape[2] // groups // sub
        piece = delta.shape[3] // shards
        count = layers * over * sub * shards * piece
        part = copies[offset : offset + count].reshape(layers, over, sub, shards, piece)
        returning.append(part.transpose(3, 0, 2, 1, 4).reshape(shards, layers, sub, over * piece))
        offset = offset + count
    back = lax.all_to_all(jnp.concatenate(returning, axis=3), "shard", split_axis=0, concat_axis=0, tiled=True)
    at = 0
    panels = []
    for delta in deltas:
        over = delta.shape[2] // groups // sub
        piece = delta.shape[3] // shards
        part = back[..., at : at + over * piece].reshape(shards, layers, sub, over, piece)
        part = part.transpose(3, 1, 2, 0, 4).reshape(over, layers, sub, -1, width)
        panels.append(part.transpose(0, 3, 1, 2, 4).reshape(-1, layers, sub, width))
        at = at + over * piece
    fresh = [jnp.zeros(delta.shape[1:], jnp.bfloat16) for delta in deltas]
    for block, whole in line_gather(jnp.concatenate(panels)):
        for kind, part in enumerate(pieces(whole)):
            part = part.reshape(layers, -1, part.shape[3])
            fresh[kind] = lax.dynamic_update_slice_in_dim(fresh[kind], part, block * part.shape[1], 1)

    mine = line_sum(lambda block: lax.dynamic_slice_in_dim(kept, block * rows, rows, 1)) / groups
    sent = mine.astype(jnp.bfloat16)
    other = lax.ppermute(sent, "tp", swap)

    def both(one, two):
        return jnp.where(side == 0, jnp.concatenate([one, two]), jnp.concatenate([two, one]))

    coefficients = both(sent, other).astype(jnp.float32)
    next_embed_momentum = MOMENTUM * embed_momentum[0, 0].T + coefficients
    direction = coefficients + MOMENTUM * next_embed_momentum

    def update(toward, precision):
        return OUTER_RATE * lax.dot_general(
            toward, basis, (((0,), (1,)), ((), ())), precision=precision, preferred_element_type=jnp.float32
        )

    next_embed = embed_owner[0, 0] - update(direction, lax.Precision.HIGHEST)
    half = lax.dynamic_slice_in_dim(direction, side * half_rank, half_rank, 0).astype(jnp.bfloat16)
    gathered = line_gather(half)
    here = jnp.concatenate([part for _, part in gathered[1:]])
    there = lax.ppermute(here, "tp", swap)
    fresh_embed = jnp.zeros((groups * rows, embed_owner.shape[3]), jnp.bfloat16)
    fresh_embed = lax.dynamic_update_slice_in_dim(
        fresh_embed, next_embed.astype(jnp.bfloat16), gathered[0][0] * rows, 0
    )
    for place, (block, part) in enumerate(gathered[1:]):
        toward = both(part, there[place * half_rank : (place + 1) * half_rank]).astype(jnp.float32)
        old = lax.dynamic_index_in_dim(all_rows, block, 0, False)
        new = old.astype(jnp.float32) - update(toward, lax.Precision.DEFAULT)
        fresh_embed = lax.dynamic_update_slice_in_dim(fresh_embed, new.astype(jnp.bfloat16), block * rows, 0)
    return (
        fresh[0],
        fresh[1],
        fresh[2],
        fresh[3],
        next_weights,
        next_momentum,
        fresh_embed,
        next_embed[None, None],
        next_embed_momentum.T[None, None],
    )


def solution(mesh):
    in_specs = (
        P("rep", None, "shard", "tp"),
        P("rep", None, "shard", "tp"),
        P("rep", None, "shard", "tp"),
        P("rep", None, "shard", "tp"),
        P("rep", "shard", "tp", None),
        P("rep", "shard", "tp", None),
        P("rep", "shard", "tp"),
        P("shard", "rep", None, "tp"),
        P("shard", "rep", None, None),
        P("tp", None),
    )
    out_specs = (
        P(None, "shard", "tp"),
        P(None, "shard", "tp"),
        P(None, "shard", "tp"),
        P(None, "shard", "tp"),
        P("rep", "shard", "tp", None),
        P("rep", "shard", "tp", None),
        P("shard", "tp"),
        P("shard", "rep", None, "tp"),
        P("shard", "rep", None, None),
    )
    return jax.shard_map(local, mesh=mesh, in_specs=in_specs, out_specs=out_specs, check_vma=False)
```

```python
import functools

import jax
import jax.numpy as jnp
from jax import lax
from jax.experimental import pallas as pl
from jax.experimental.pallas import tpu as pltpu
from jax.sharding import PartitionSpec as P

MOMENTUM = 0.5
OUTER_RATE = 0.7
LANES = 128

OUT_IN = [(0, 1), (3, 2)]
MIDDLE = [(1, 2), (2, 1)]
IN_OUT = [(1, 0), (2, 3)]
NEAR = OUT_IN + IN_OUT
SWAP = [(0, 1), (1, 0)]


def permute(value, pairs):
    return lax.ppermute(value, "rep", pairs)


def wide(value):
    return value.astype(jnp.float32)


def add(one, two):
    return (wide(one) + wide(two)).astype(one.dtype)


def at_end():
    rank = lax.axis_index("rep")
    return (rank == 0) | (rank == 3)


def block_of(place):
    return jnp.where(lax.axis_index("rep") >= 2, 3 - place, place)


def block_at(step):
    if step == 0:
        return lax.axis_index("rep")
    return block_of(jnp.where(at_end(), 1, 0)) if step == 1 else block_of(step)


class Kind:
    def __init__(self, delta, groups, shards, sub, width, panel, column):
        self.layers, self.rows, self.cols = delta.shape[1:]
        self.count = self.rows // groups
        self.over = self.count // sub
        self.across = self.cols // width
        self.piece = self.cols // shards
        self.panel = panel
        self.column = column


def make_kinds(deltas, groups, shards):
    width = min(delta.shape[3] for delta in deltas)
    sub = min(delta.shape[2] for delta in deltas) // groups
    kinds = []
    panel = column = 0
    for delta in deltas:
        kind = Kind(delta, groups, shards, sub, width, panel, column)
        kinds.append(kind)
        panel = panel + kind.over * kind.across
        column = column + kind.over * kind.piece
    return kinds, sub, width, panel, column


def each_panel(kinds, sub, width):
    for index, kind in enumerate(kinds):
        for group in range(kind.over):
            for across in range(kind.across):
                panel = kind.panel + group * kind.across + across
                for layer in range(kind.layers):
                    yield index, layer, group * sub, across * width, panel, layer * sub


def pack_kernel(kinds, sub, width, *refs):
    deltas, blocks, sem = refs[: len(kinds)], refs[len(kinds) : -1], refs[-1]
    for order, target in enumerate(blocks):
        block = block_of(len(blocks) - 1 - order)
        for index, layer, row, column, panel, at in each_panel(kinds, sub, width):
            start = pl.multiple_of(block * kinds[index].count + row, 16)
            source = deltas[index].at[0, layer, pl.ds(start, sub), pl.ds(column, width)]
            pltpu.make_async_copy(source, target.at[panel, pl.ds(at, sub), :], sem.at[order]).start()
    for order, target in enumerate(blocks):
        pltpu.make_async_copy(target, target, sem.at[order]).wait()


def place_kernel(kinds, sub, width, step, *refs):
    one, two = refs[:2]
    fresh, sem = refs[-1 - len(kinds) : -1], refs[-1]
    block = block_at(step)

    def start(source):
        for index, layer, row, column, panel, at in each_panel(kinds, sub, width):
            first = pl.multiple_of(block * kinds[index].count + row, 16)
            target = fresh[index].at[layer, pl.ds(first, sub), pl.ds(column, width)]
            pltpu.make_async_copy(source.at[panel, pl.ds(at, sub), :], target, sem).start()

    pl.when(at_end())(lambda: start(one))
    pl.when(jnp.logical_not(at_end()))(lambda: start(two))
    pltpu.make_async_copy(one, one, sem).wait()


def split_kernel(kinds, width, shards, near, last, from_out, from_middle, from_in, *refs):
    end, pieces = at_end(), refs[-1]
    for kind in kinds:
        for group in range(kind.over):
            parts = []
            for across in range(kind.across):
                panel = kind.panel + group * kind.across + across
                mine = jnp.where(end, wide(last[panel]), wide(near[panel]))
                arrived = wide(from_out[panel]) + wide(from_middle[panel]) + wide(from_in[panel])
                parts.append(mine + arrived)
            whole = jnp.concatenate(parts, axis=1)
            column = kind.column + group * kind.piece
            for s in range(shards):
                part = whole[:, s * kind.piece : (s + 1) * kind.piece]
                pieces[s, :, column : column + kind.piece] = part.astype(pieces.dtype)


def join_kernel(kinds, width, shards, pieces, *refs):
    panels = refs[-1]
    wholes = [wide(pieces[s]) for s in range(shards)]
    for kind in kinds:
        for group in range(kind.over):
            column = kind.column + group * kind.piece
            whole = jnp.concatenate([part[:, column : column + kind.piece] for part in wholes], axis=1)
            for across in range(kind.across):
                panel = kind.panel + group * kind.across + across
                panels[panel] = whole[:, across * width : (across + 1) * width].astype(panels.dtype)


def owner_update_kernel(units, shards, groups, moved, weights, momentum, *refs):
    next_weights, next_momentum, back = refs[-3:]
    for flat, row, rows, column, piece in units:
        here = slice(row, row + rows)
        parts = [moved[s, here, :].astype(jnp.float32)[:, column : column + piece] for s in range(shards)]
        gradient = jnp.concatenate(parts, axis=1) / groups
        tiles = shards * piece // LANES
        fresh = []
        for tile in range(tiles):
            at = pl.ds(flat + tile, rows, stride=tiles)
            grad = gradient[:, tile * LANES : (tile + 1) * LANES]
            new_momentum = MOMENTUM * momentum[at, :] + grad
            new_weights = weights[at, :] - OUTER_RATE * (grad + MOMENTUM * new_momentum)
            next_momentum[at, :] = new_momentum
            next_weights[at, :] = new_weights
            fresh.append(new_weights)
        fresh = jnp.concatenate(fresh, axis=1)
        for s in range(shards):
            back[s, here, column : column + piece] = fresh[:, s * piece : (s + 1) * piece].astype(back.dtype)


def kernel_call(body, out_shape, moved_bytes, **more):
    return pl.pallas_call(
        body,
        out_shape=out_shape,
        compiler_params=pltpu.CompilerParams(vmem_limit_bytes=40 << 20),
        cost_estimate=pl.CostEstimate(flops=0, bytes_accessed=moved_bytes, transcendentals=0),
        **more,
    )


ANYWHERE = pl.BlockSpec(memory_space=pl.ANY)
IN_VMEM = pl.BlockSpec(memory_space=pltpu.VMEM)


def copy_kernel(value, *refs):
    refs[-1][...] = value[...]


def after(value, *others):
    return kernel_call(
        copy_kernel,
        jax.ShapeDtypeStruct(value.shape, value.dtype),
        2 * value.size * value.dtype.itemsize,
        in_specs=[IN_VMEM] + [ANYWHERE] * len(others),
    )(value, *others)


def hold_kernel(*refs):
    pass


def hold(value, *others):
    return kernel_call(
        hold_kernel,
        jax.ShapeDtypeStruct(value.shape, value.dtype),
        0,
        in_specs=[ANYWHERE] * (1 + len(others)),
        out_specs=ANYWHERE,
        input_output_aliases={0: 0},
    )(value, *others)


def add_kernel(count, *refs):
    for one, two, total in zip(refs[:count], refs[count : 2 * count], refs[-count:]):
        total[...] = (wide(one[...]) + wide(two[...])).astype(total.dtype)


def add_after(pairs, *others):
    count = len(pairs)
    return kernel_call(
        functools.partial(add_kernel, count),
        [jax.ShapeDtypeStruct(one.shape, one.dtype) for one, _ in pairs],
        6 * sum(one.size for one, _ in pairs),
        in_specs=[IN_VMEM] * (2 * count) + [ANYWHERE] * len(others),
    )(*[one for one, _ in pairs], *[two for _, two in pairs], *others)


def narrow_kernel(cut, wide_rows, low, high):
    low[...] = wide_rows[:cut, :].astype(low.dtype)
    high[...] = wide_rows[cut:, :].astype(high.dtype)


def narrow_rows(array, cut):
    rows, columns = array.shape[2:]
    if cut % 16 or rows % 8:
        return [part.astype(jnp.bfloat16) for part in (array[0, 0, :cut], array[0, 0, cut:])]
    return kernel_call(
        functools.partial(narrow_kernel, cut),
        [jax.ShapeDtypeStruct((count, columns), jnp.bfloat16) for count in (cut, rows - cut)],
        6 * rows * columns,
    )(array.reshape(rows, columns))


class Dense:
    def __init__(self, deltas, groups, shards):
        self.groups, self.shards = groups, shards
        self.kinds, self.sub, self.width, self.panels, self.columns = make_kinds(deltas, groups, shards)
        self.layers = deltas[0].shape[1]
        self.dtype = deltas[0].dtype
        self.block_shape = (self.panels, self.layers * self.sub, self.width)
        self.block_bytes = 2 * self.panels * self.layers * self.sub * self.width
        self.aligned = self.sub % 16 == 0 and self.width % LANES == 0
        self.aligned = self.aligned and all(shards * kind.piece % LANES == 0 for kind in self.kinds)

    def pack(self, deltas):
        if self.aligned:
            return kernel_call(
                functools.partial(pack_kernel, self.kinds, self.sub, self.width),
                [jax.ShapeDtypeStruct(self.block_shape, self.dtype)] * 4,
                8 * self.block_bytes,
                in_specs=[ANYWHERE] * len(deltas),
                out_specs=[ANYWHERE] * 4,
                scratch_shapes=[pltpu.SemaphoreType.DMA((4,))],
            )(*deltas)

        def block_panels(block):
            panels = []
            for kind, delta in zip(self.kinds, deltas):
                part = lax.dynamic_slice_in_dim(delta[0], block * kind.count, kind.count, 1)
                part = part.reshape(kind.layers, kind.over, self.sub, kind.across, self.width)
                panels.append(part.transpose(1, 3, 0, 2, 4).reshape(-1, *self.block_shape[1:]))
            return jnp.concatenate(panels)

        return [block_panels(block_of(place)) for place in (3, 2, 1, 0)]

    def as_kinds(self, block):
        parts = []
        for kind in self.kinds:
            part = block[kind.panel : kind.panel + kind.over * kind.across]
            part = part.reshape(kind.over, kind.across, kind.layers, self.sub, self.width)
            parts.append(part.transpose(2, 0, 3, 1, 4).reshape(kind.layers, kind.over, self.sub, kind.cols))
        return parts

    def split(self, near, last, from_out, from_middle, from_in, *others):
        shape = (self.shards, self.layers * self.sub, self.columns)
        if self.aligned:
            return kernel_call(
                functools.partial(split_kernel, self.kinds, self.width, self.shards),
                jax.ShapeDtypeStruct(shape, self.dtype),
                9 * self.block_bytes,
                in_specs=[IN_VMEM] * 5 + [ANYWHERE] * len(others),
            )(near, last, from_out, from_middle, from_in, *others)
        mine = jnp.where(at_end(), last, near)
        total = wide(mine) + wide(from_out) + wide(from_middle) + wide(from_in)
        pieces = []
        for kind, part in zip(self.kinds, self.as_kinds(total.astype(self.dtype))):
            part = part.reshape(kind.layers, kind.over, self.sub, self.shards, kind.piece)
            pieces.append(part.transpose(3, 0, 2, 1, 4).reshape(shape[:2] + (kind.over * kind.piece,)))
        return jnp.concatenate(pieces, axis=2)

    def join(self, pieces, *others):
        if self.aligned:
            return kernel_call(
                functools.partial(join_kernel, self.kinds, self.width, self.shards),
                jax.ShapeDtypeStruct(self.block_shape, self.dtype),
                2 * self.block_bytes,
                in_specs=[IN_VMEM] + [ANYWHERE] * len(others),
            )(pieces, *others)
        panels = []
        for kind in self.kinds:
            part = pieces[..., kind.column : kind.column + kind.over * kind.piece]
            part = part.reshape(self.shards, kind.layers, self.sub, kind.over, kind.piece)
            part = part.transpose(3, 1, 2, 0, 4).reshape(kind.over, kind.layers, self.sub, kind.across, self.width)
            panels.append(part.transpose(0, 3, 1, 2, 4).reshape(-1, *self.block_shape[1:]))
        return jnp.concatenate(panels)

    def place(self, fresh, step, one, two):
        shapes = [(kind.layers, kind.rows, kind.cols) for kind in self.kinds]
        if self.aligned:
            before = fresh or []
            return kernel_call(
                functools.partial(place_kernel, self.kinds, self.sub, self.width, step),
                [jax.ShapeDtypeStruct(shape, self.dtype) for shape in shapes],
                2 * self.block_bytes,
                in_specs=[ANYWHERE] * (2 + len(before)),
                out_specs=[ANYWHERE] * len(shapes),
                scratch_shapes=[pltpu.SemaphoreType.DMA],
                input_output_aliases={2 + index: index for index in range(len(before))},
            )(one, two, *before)
        fresh = fresh or [jnp.zeros(shape, self.dtype) for shape in shapes]
        block = jnp.where(at_end(), one, two)
        placed = []
        for kind, target, part in zip(self.kinds, fresh, self.as_kinds(block)):
            part = part.reshape(kind.layers, kind.count, kind.cols)
            placed.append(lax.dynamic_update_slice_in_dim(target, part, block_at(step) * kind.count, 1))
        return placed

    def update(self, moved, weights, momentum, *others):
        if self.aligned:
            units = []
            flat = 0
            for kind in self.kinds:
                for layer in range(kind.layers):
                    for group in range(kind.over):
                        column = kind.column + group * kind.piece
                        units.append((flat, layer * self.sub, self.sub, column, kind.piece))
                        flat = flat + self.sub * self.shards * kind.piece // LANES
            flat_shape = jax.ShapeDtypeStruct((flat, LANES), jnp.float32)
            next_weights, next_momentum, back = kernel_call(
                functools.partial(owner_update_kernel, units, self.shards, self.groups),
                (flat_shape, flat_shape, jax.ShapeDtypeStruct(moved.shape, moved.dtype)),
                10 * self.block_bytes,
                in_specs=[IN_VMEM] * 3 + [ANYWHERE] * len(others),
            )(moved, weights.reshape(flat, LANES), momentum.reshape(flat, LANES), *others)
            return next_weights.reshape(weights.shape), next_momentum.reshape(weights.shape), back
        flats = []
        for kind in self.kinds:
            part = moved[..., kind.column : kind.column + kind.over * kind.piece]
            part = part.reshape(self.shards, kind.layers, self.sub, kind.over, kind.piece)
            flats.append(part.transpose(1, 3, 2, 0, 4).reshape(-1))
        gradient = (wide(jnp.concatenate(flats)) / self.groups).reshape(weights.shape)
        next_momentum = MOMENTUM * momentum + gradient
        next_weights = weights - OUTER_RATE * (gradient + MOMENTUM * next_momentum)
        copies = next_weights.astype(moved.dtype).reshape(-1)
        returning = []
        at = 0
        for kind in self.kinds:
            count = kind.layers * kind.count * kind.cols
            part = copies[at : at + count].reshape(kind.layers, kind.over, self.sub, self.shards, kind.piece)
            returning.append(part.transpose(3, 0, 2, 1, 4).reshape(moved.shape[:2] + (kind.over * kind.piece,)))
            at = at + count
        return next_weights, next_momentum, jnp.concatenate(returning, axis=2)


def local(
    delta_inputs,
    delta_mixing,
    delta_expand,
    delta_reduce,
    owner_weights,
    owner_momentum,
    delta_embed,
    embed_owner,
    embed_momentum,
    basis,
):
    groups = lax.axis_size("rep")
    shards = lax.axis_size("shard")
    side = lax.axis_index("tp")
    end = at_end()
    deltas = (delta_inputs, delta_mixing, delta_expand, delta_reduce)
    dense = Dense(deltas, groups, shards)


    def to_end(value):
        return permute(value, IN_OUT)

    def across(value):
        return permute(value, MIDDLE)

    def to_inner(value):
        return permute(value, OUT_IN)

    rows = embed_owner.shape[2]
    half_rank = basis.shape[1] // 2
    cut = rows // 2 // LANES * LANES
    low, high = narrow_rows(embed_owner, cut)
    rows_near = [to_end(low), to_end(high)]
    rows_across = [across(low), across(high)]
    rows_far = [to_end(part) for part in rows_across]

    far, middle, near, last = dense.pack(deltas)
    far_in, middle_in, near_in = (to_inner(part) for part in (far, middle, near))
    (far_sum,) = add_after([(far, far_in)], rows_near[0], rows_across[0])
    far_across = across(far_sum)
    middle_sum, last_sum = add_after([(middle, middle_in), (last, far_across)], rows_near[1])
    middle_across = across(middle_sum)
    last_out = to_end(last_sum)
    rows_inner = [to_inner(low)]
    pieces = dense.split(
        near, last, near_in, middle_across, last_out, rows_far[0], rows_across[1], rows_inner[0]
    )
    rows_inner.append(to_inner(hold(high, pieces)))
    rows_across_2 = [across(part) for part in rows_inner]
    rows_last = [to_end(part) for part in rows_across_2]

    terms = lax.dot_general(
        after(basis, far),
        wide(delta_embed[0]),
        (((0,), (1,)), ((), ())),
        precision=lax.Precision.HIGH,
        preferred_element_type=jnp.float32,
    ).astype(jnp.bfloat16)
    keep = lax.dynamic_slice_in_dim(terms, side * half_rank, half_rank, 0)
    give = lax.dynamic_slice_in_dim(terms, (1 - side) * half_rank, half_rank, 0)
    (kept,) = add_after([(keep, lax.ppermute(give, "tp", SWAP))], pieces)

    def term(place):
        return lax.dynamic_slice_in_dim(kept, block_of(place) * rows, rows, 1)

    terms_out = to_inner(jnp.stack([term(3), term(2), term(1)]))
    terms_middle = across(jnp.stack([add(term(3), terms_out[0]), add(term(2), terms_out[1])]))
    terms_in = to_end(add(term(0), terms_middle[0]))

    moved = lax.all_to_all(pieces, "shard", split_axis=0, concat_axis=0, tiled=True)
    next_weights, next_momentum, back = dense.update(moved, owner_weights, owner_momentum, terms_out)
    back = lax.all_to_all(back, "shard", split_axis=0, concat_axis=0, tiled=True)
    new_block = dense.join(back, rows_far[1], rows_across_2[0], terms_middle)

    mine = jnp.where(end, term(0), term(1))
    total = wide(mine) + wide(terms_out[2]) + wide(terms_middle[1]) + wide(terms_in)
    sent = (total / groups).astype(jnp.bfloat16)
    other = lax.ppermute(sent, "tp", SWAP)

    def both(one, two):
        return jnp.where(side == 0, jnp.concatenate([one, two]), jnp.concatenate([two, one]))

    coefficients = wide(both(sent, other))
    next_embed_momentum = MOMENTUM * embed_momentum[0, 0].T + coefficients
    direction = coefficients + MOMENTUM * next_embed_momentum

    def update(toward, precision):
        return OUTER_RATE * lax.dot_general(
            toward, basis, (((0,), (1,)), ((), ())), precision=precision, preferred_element_type=jnp.float32
        )

    next_embed = embed_owner[0, 0] - update(direction, lax.Precision.HIGHEST)
    half = lax.dynamic_slice_in_dim(direction, side * half_rank, half_rank, 0).astype(jnp.bfloat16)

    rank = lax.axis_index("rep")
    halves = jnp.stack([permute(half, [(i, (i + step) % groups) for i in range(groups)]) for step in (1, 2, 3)])
    others = lax.ppermute(halves, "tp", SWAP)
    block_near = permute(new_block, NEAR)
    block_across = across(new_block)
    block_across = hold(block_across, rows_inner[1], rows_last[0], terms_in)
    block_far = to_end(block_across)
    block_across_2 = hold(across(block_near), rows_across_2[1], others)
    block_last = to_end(block_across_2)

    fresh = dense.place(None, 0, new_block, new_block)
    fresh = dense.place(fresh, 1, block_near, block_near)
    fresh = dense.place(fresh, 2, block_far, block_across)
    fresh = dense.place(fresh, 3, block_last, block_across_2)

    fresh_embed = jnp.zeros((groups * rows, embed_owner.shape[3]), jnp.bfloat16)

    def put(target, value, step, start):
        return lax.dynamic_update_slice_in_dim(target, value.astype(target.dtype), block_at(step) * rows + start, 0)

    fresh_embed = put(fresh_embed, next_embed, 0, 0)
    arrived = [(1, rows_near, rows_inner), (2, rows_far, rows_across), (3, rows_last, rows_across_2)]
    for step, at_ends, inside in arrived:
        back_by = (rank - block_at(step) - 1) % groups
        here, there = (lax.dynamic_index_in_dim(part, back_by, 0, False) for part in (halves, others))
        toward = both(here, there)
        for start, one, two in zip((0, cut), at_ends, inside):
            part = jnp.where(end, one, two)
            change = update(wide(toward[:, start : start + part.shape[0]]), lax.Precision.DEFAULT)
            fresh_embed = put(fresh_embed, wide(part) - change, step, start)
    return (
        fresh[0],
        fresh[1],
        fresh[2],
        fresh[3],
        next_weights,
        next_momentum,
        fresh_embed,
        next_embed[None, None],
        next_embed_momentum.T[None, None],
    )


def solution(mesh):
    in_specs = (
        P("rep", None, "shard", "tp"),
        P("rep", None, "shard", "tp"),
        P("rep", None, "shard", "tp"),
        P("rep", None, "shard", "tp"),
        P("rep", "shard", "tp", None),
        P("rep", "shard", "tp", None),
        P("rep", "shard", "tp"),
        P("shard", "rep", None, "tp"),
        P("shard", "rep", None, None),
        P("tp", None),
    )
    out_specs = (
        P(None, "shard", "tp"),
        P(None, "shard", "tp"),
        P(None, "shard", "tp"),
        P(None, "shard", "tp"),
        P("rep", "shard", "tp", None),
        P("rep", "shard", "tp", None),
        P("shard", "tp"),
        P("shard", "rep", None, "tp"),
        P("shard", "rep", None, None),
    )
    return jax.shard_map(local, mesh=mesh, in_specs=in_specs, out_specs=out_specs, check_vma=False)
```

```python
import functools

import jax
import jax.numpy as jnp
from jax import lax
from jax.experimental import pallas as pl
from jax.experimental.pallas import tpu as pltpu
from jax.sharding import PartitionSpec as P

MOMENTUM = 0.5
OUTER_RATE = 0.7
LANES = 128

OUT_IN = [(0, 1), (3, 2)]
MIDDLE = [(1, 2), (2, 1)]
IN_OUT = [(1, 0), (2, 3)]
NEAR = OUT_IN + IN_OUT
SWAP = [(0, 1), (1, 0)]


def permute(value, pairs):
    return lax.ppermute(value, "rep", pairs)


def wide(value):
    return value.astype(jnp.float32)


def add(one, two):
    return (wide(one) + wide(two)).astype(one.dtype)


def at_end():
    rank = lax.axis_index("rep")
    return (rank == 0) | (rank == 3)


def block_of(place):
    return jnp.where(lax.axis_index("rep") >= 2, 3 - place, place)


def block_at(step):
    if step == 0:
        return lax.axis_index("rep")
    return block_of(jnp.where(at_end(), 1, 0)) if step == 1 else block_of(step)


class Kind:
    def __init__(self, delta, groups, shards, sub, width, panel, column):
        self.layers, self.rows, self.cols = delta.shape[1:]
        self.count = self.rows // groups
        self.over = self.count // sub
        self.across = self.cols // width
        self.piece = self.cols // shards
        self.panel = panel
        self.column = column


def make_kinds(deltas, groups, shards):
    width = min(delta.shape[3] for delta in deltas)
    sub = min(delta.shape[2] for delta in deltas) // groups
    kinds = []
    panel = column = 0
    for delta in deltas:
        kind = Kind(delta, groups, shards, sub, width, panel, column)
        kinds.append(kind)
        panel = panel + kind.over * kind.across
        column = column + kind.over * kind.piece
    return kinds, sub, width, panel, column


def each_panel(kinds, sub, width):
    for index, kind in enumerate(kinds):
        for group in range(kind.over):
            for across in range(kind.across):
                panel = kind.panel + group * kind.across + across
                for layer in range(kind.layers):
                    yield index, layer, group * sub, across * width, panel, layer * sub


def pack_kernel(kinds, sub, width, *refs):
    deltas, blocks, sem = refs[: len(kinds)], refs[len(kinds) : -1], refs[-1]
    for order, target in enumerate(blocks):
        block = block_of(len(blocks) - 1 - order)
        for index, layer, row, column, panel, at in each_panel(kinds, sub, width):
            start = pl.multiple_of(block * kinds[index].count + row, 16)
            source = deltas[index].at[0, layer, pl.ds(start, sub), pl.ds(column, width)]
            pltpu.make_async_copy(source, target.at[panel, pl.ds(at, sub), :], sem.at[order]).start()
    for order, target in enumerate(blocks):
        pltpu.make_async_copy(target, target, sem.at[order]).wait()


def place_kernel(kinds, sub, width, step, *refs):
    one, two = refs[:2]
    fresh, sem = refs[-1 - len(kinds) : -1], refs[-1]
    block = block_at(step)

    def start(source):
        for index, layer, row, column, panel, at in each_panel(kinds, sub, width):
            first = pl.multiple_of(block * kinds[index].count + row, 16)
            target = fresh[index].at[layer, pl.ds(first, sub), pl.ds(column, width)]
            pltpu.make_async_copy(source.at[panel, pl.ds(at, sub), :], target, sem).start()

    pl.when(at_end())(lambda: start(one))
    pl.when(jnp.logical_not(at_end()))(lambda: start(two))
    pltpu.make_async_copy(one, one, sem).wait()


def split_kernel(kinds, width, shards, near, last, from_out, from_middle, from_in, *refs):
    end, pieces = at_end(), refs[-1]
    for kind in kinds:
        for group in range(kind.over):
            parts = []
            for across in range(kind.across):
                panel = kind.panel + group * kind.across + across
                mine = jnp.where(end, wide(last[panel]), wide(near[panel]))
                arrived = wide(from_out[panel]) + wide(from_middle[panel]) + wide(from_in[panel])
                parts.append(mine + arrived)
            whole = jnp.concatenate(parts, axis=1)
            column = kind.column + group * kind.piece
            for s in range(shards):
                part = whole[:, s * kind.piece : (s + 1) * kind.piece]
                pieces[s, :, column : column + kind.piece] = part.astype(pieces.dtype)


def join_kernel(kinds, width, shards, pieces, *refs):
    panels = refs[-1]
    wholes = [wide(pieces[s]) for s in range(shards)]
    for kind in kinds:
        for group in range(kind.over):
            column = kind.column + group * kind.piece
            whole = jnp.concatenate([part[:, column : column + kind.piece] for part in wholes], axis=1)
            for across in range(kind.across):
                panel = kind.panel + group * kind.across + across
                panels[panel] = whole[:, across * width : (across + 1) * width].astype(panels.dtype)


def owner_update_kernel(units, shards, groups, moved, weights, momentum, *refs):
    next_weights, next_momentum, back = refs[-3:]
    for flat, row, rows, column, piece in units:
        here = slice(row, row + rows)
        parts = [moved[s, here, :].astype(jnp.float32)[:, column : column + piece] for s in range(shards)]
        gradient = jnp.concatenate(parts, axis=1) / groups
        tiles = shards * piece // LANES
        fresh = []
        for tile in range(tiles):
            at = pl.ds(flat + tile, rows, stride=tiles)
            grad = gradient[:, tile * LANES : (tile + 1) * LANES]
            new_momentum = MOMENTUM * momentum[at, :] + grad
            new_weights = weights[at, :] - OUTER_RATE * (grad + MOMENTUM * new_momentum)
            next_momentum[at, :] = new_momentum
            next_weights[at, :] = new_weights
            fresh.append(new_weights)
        fresh = jnp.concatenate(fresh, axis=1)
        for s in range(shards):
            back[s, here, column : column + piece] = fresh[:, s * piece : (s + 1) * piece].astype(back.dtype)


def kernel_call(body, out_shape, moved_bytes, **more):
    return pl.pallas_call(
        body,
        out_shape=out_shape,
        compiler_params=pltpu.CompilerParams(vmem_limit_bytes=40 << 20),
        cost_estimate=pl.CostEstimate(flops=0, bytes_accessed=moved_bytes, transcendentals=0),
        **more,
    )


ANYWHERE = pl.BlockSpec(memory_space=pl.ANY)
IN_VMEM = pl.BlockSpec(memory_space=pltpu.VMEM)


def copy_kernel(value, *refs):
    refs[-1][...] = value[...]


def after(value, *others):
    return kernel_call(
        copy_kernel,
        jax.ShapeDtypeStruct(value.shape, value.dtype),
        2 * value.size * value.dtype.itemsize,
        in_specs=[IN_VMEM] + [ANYWHERE] * len(others),
    )(value, *others)


def hold_kernel(*refs):
    pass


def hold(value, *others):
    return kernel_call(
        hold_kernel,
        jax.ShapeDtypeStruct(value.shape, value.dtype),
        0,
        in_specs=[ANYWHERE] * (1 + len(others)),
        out_specs=ANYWHERE,
        input_output_aliases={0: 0},
    )(value, *others)


def add_kernel(count, *refs):
    for one, two, total in zip(refs[:count], refs[count : 2 * count], refs[-count:]):
        total[...] = (wide(one[...]) + wide(two[...])).astype(total.dtype)


def add_after(pairs, *others):
    count = len(pairs)
    return kernel_call(
        functools.partial(add_kernel, count),
        [jax.ShapeDtypeStruct(one.shape, one.dtype) for one, _ in pairs],
        6 * sum(one.size for one, _ in pairs),
        in_specs=[IN_VMEM] * (2 * count) + [ANYWHERE] * len(others),
    )(*[one for one, _ in pairs], *[two for _, two in pairs], *others)


def mean_kernel(count, groups, *refs):
    refs[-1][...] = (sum(wide(ref[...]) for ref in refs[:count]) / groups).astype(refs[-1].dtype)


def mean_after(groups, terms, *others):
    return kernel_call(
        functools.partial(mean_kernel, len(terms), groups),
        jax.ShapeDtypeStruct(terms[0].shape, terms[0].dtype),
        10 * terms[0].size,
        in_specs=[IN_VMEM] * len(terms) + [ANYWHERE] * len(others),
    )(*terms, *others)


def narrow_kernel(cut, wide_rows, low, high):
    low[...] = wide_rows[:cut, :].astype(low.dtype)
    high[...] = wide_rows[cut:, :].astype(high.dtype)


def narrow_rows(array, cut):
    rows, columns = array.shape[2:]
    if cut % 16 or rows % 8:
        return [part.astype(jnp.bfloat16) for part in (array[0, 0, :cut], array[0, 0, cut:])]
    return kernel_call(
        functools.partial(narrow_kernel, cut),
        [jax.ShapeDtypeStruct((count, columns), jnp.bfloat16) for count in (cut, rows - cut)],
        6 * rows * columns,
    )(array.reshape(rows, columns))


class Dense:
    def __init__(self, deltas, groups, shards):
        self.groups, self.shards = groups, shards
        self.kinds, self.sub, self.width, self.panels, self.columns = make_kinds(deltas, groups, shards)
        self.layers = deltas[0].shape[1]
        self.dtype = deltas[0].dtype
        self.block_shape = (self.panels, self.layers * self.sub, self.width)
        self.block_bytes = 2 * self.panels * self.layers * self.sub * self.width
        self.aligned = self.sub % 16 == 0 and self.width % LANES == 0
        self.aligned = self.aligned and all(shards * kind.piece % LANES == 0 for kind in self.kinds)

    def pack(self, deltas):
        if self.aligned:
            return kernel_call(
                functools.partial(pack_kernel, self.kinds, self.sub, self.width),
                [jax.ShapeDtypeStruct(self.block_shape, self.dtype)] * 4,
                8 * self.block_bytes,
                in_specs=[ANYWHERE] * len(deltas),
                out_specs=[ANYWHERE] * 4,
                scratch_shapes=[pltpu.SemaphoreType.DMA((4,))],
            )(*deltas)

        def block_panels(block):
            panels = []
            for kind, delta in zip(self.kinds, deltas):
                part = lax.dynamic_slice_in_dim(delta[0], block * kind.count, kind.count, 1)
                part = part.reshape(kind.layers, kind.over, self.sub, kind.across, self.width)
                panels.append(part.transpose(1, 3, 0, 2, 4).reshape(-1, *self.block_shape[1:]))
            return jnp.concatenate(panels)

        return [block_panels(block_of(place)) for place in (3, 2, 1, 0)]

    def as_kinds(self, block):
        parts = []
        for kind in self.kinds:
            part = block[kind.panel : kind.panel + kind.over * kind.across]
            part = part.reshape(kind.over, kind.across, kind.layers, self.sub, self.width)
            parts.append(part.transpose(2, 0, 3, 1, 4).reshape(kind.layers, kind.over, self.sub, kind.cols))
        return parts

    def split(self, near, last, from_out, from_middle, from_in, *others):
        shape = (self.shards, self.layers * self.sub, self.columns)
        if self.aligned:
            return kernel_call(
                functools.partial(split_kernel, self.kinds, self.width, self.shards),
                jax.ShapeDtypeStruct(shape, self.dtype),
                9 * self.block_bytes,
                in_specs=[IN_VMEM] * 5 + [ANYWHERE] * len(others),
            )(near, last, from_out, from_middle, from_in, *others)
        mine = jnp.where(at_end(), last, near)
        total = wide(mine) + wide(from_out) + wide(from_middle) + wide(from_in)
        pieces = []
        for kind, part in zip(self.kinds, self.as_kinds(total.astype(self.dtype))):
            part = part.reshape(kind.layers, kind.over, self.sub, self.shards, kind.piece)
            pieces.append(part.transpose(3, 0, 2, 1, 4).reshape(shape[:2] + (kind.over * kind.piece,)))
        return jnp.concatenate(pieces, axis=2)

    def join(self, pieces, *others):
        if self.aligned:
            return kernel_call(
                functools.partial(join_kernel, self.kinds, self.width, self.shards),
                jax.ShapeDtypeStruct(self.block_shape, self.dtype),
                2 * self.block_bytes,
                in_specs=[IN_VMEM] + [ANYWHERE] * len(others),
            )(pieces, *others)
        panels = []
        for kind in self.kinds:
            part = pieces[..., kind.column : kind.column + kind.over * kind.piece]
            part = part.reshape(self.shards, kind.layers, self.sub, kind.over, kind.piece)
            part = part.transpose(3, 1, 2, 0, 4).reshape(kind.over, kind.layers, self.sub, kind.across, self.width)
            panels.append(part.transpose(0, 3, 1, 2, 4).reshape(-1, *self.block_shape[1:]))
        return jnp.concatenate(panels)

    def place(self, fresh, step, one, two):
        shapes = [(kind.layers, kind.rows, kind.cols) for kind in self.kinds]
        if self.aligned:
            before = fresh or []
            return kernel_call(
                functools.partial(place_kernel, self.kinds, self.sub, self.width, step),
                [jax.ShapeDtypeStruct(shape, self.dtype) for shape in shapes],
                2 * self.block_bytes,
                in_specs=[ANYWHERE] * (2 + len(before)),
                out_specs=[ANYWHERE] * len(shapes),
                scratch_shapes=[pltpu.SemaphoreType.DMA],
                input_output_aliases={2 + index: index for index in range(len(before))},
            )(one, two, *before)
        fresh = fresh or [jnp.zeros(shape, self.dtype) for shape in shapes]
        block = jnp.where(at_end(), one, two)
        placed = []
        for kind, target, part in zip(self.kinds, fresh, self.as_kinds(block)):
            part = part.reshape(kind.layers, kind.count, kind.cols)
            placed.append(lax.dynamic_update_slice_in_dim(target, part, block_at(step) * kind.count, 1))
        return placed

    def update(self, moved, weights, momentum, *others):
        if self.aligned:
            units = []
            flat = 0
            for kind in self.kinds:
                for layer in range(kind.layers):
                    for group in range(kind.over):
                        column = kind.column + group * kind.piece
                        units.append((flat, layer * self.sub, self.sub, column, kind.piece))
                        flat = flat + self.sub * self.shards * kind.piece // LANES
            flat_shape = jax.ShapeDtypeStruct((flat, LANES), jnp.float32)
            next_weights, next_momentum, back = kernel_call(
                functools.partial(owner_update_kernel, units, self.shards, self.groups),
                (flat_shape, flat_shape, jax.ShapeDtypeStruct(moved.shape, moved.dtype)),
                10 * self.block_bytes,
                in_specs=[IN_VMEM] * 3 + [ANYWHERE] * len(others),
            )(moved, weights.reshape(flat, LANES), momentum.reshape(flat, LANES), *others)
            return next_weights.reshape(weights.shape), next_momentum.reshape(weights.shape), back
        flats = []
        for kind in self.kinds:
            part = moved[..., kind.column : kind.column + kind.over * kind.piece]
            part = part.reshape(self.shards, kind.layers, self.sub, kind.over, kind.piece)
            flats.append(part.transpose(1, 3, 2, 0, 4).reshape(-1))
        gradient = (wide(jnp.concatenate(flats)) / self.groups).reshape(weights.shape)
        next_momentum = MOMENTUM * momentum + gradient
        next_weights = weights - OUTER_RATE * (gradient + MOMENTUM * next_momentum)
        copies = next_weights.astype(moved.dtype).reshape(-1)
        returning = []
        at = 0
        for kind in self.kinds:
            count = kind.layers * kind.count * kind.cols
            part = copies[at : at + count].reshape(kind.layers, kind.over, self.sub, self.shards, kind.piece)
            returning.append(part.transpose(3, 0, 2, 1, 4).reshape(moved.shape[:2] + (kind.over * kind.piece,)))
            at = at + count
        return next_weights, next_momentum, jnp.concatenate(returning, axis=2)


def local(
    delta_inputs,
    delta_mixing,
    delta_expand,
    delta_reduce,
    owner_weights,
    owner_momentum,
    delta_embed,
    embed_owner,
    embed_momentum,
    basis,
):
    groups = lax.axis_size("rep")
    shards = lax.axis_size("shard")
    side = lax.axis_index("tp")
    end = at_end()
    deltas = (delta_inputs, delta_mixing, delta_expand, delta_reduce)
    dense = Dense(deltas, groups, shards)


    def to_end(value):
        return permute(value, IN_OUT)

    def across(value):
        return permute(value, MIDDLE)

    def to_inner(value):
        return permute(value, OUT_IN)

    rows = embed_owner.shape[2]
    half_rank = basis.shape[1] // 2
    cut = rows // 2 // LANES * LANES
    low, high = narrow_rows(embed_owner, cut)
    rows_near = [to_end(low), to_end(high)]
    rows_across = [across(low), across(high)]
    rows_far = [to_end(part) for part in rows_across]

    far, middle, near, last = dense.pack(deltas)
    far_in, middle_in, near_in = (to_inner(part) for part in (far, middle, near))
    (far_sum,) = add_after([(far, far_in)], rows_near[0], rows_across[0])
    far_across = across(far_sum)
    middle_sum, last_sum = add_after([(middle, middle_in), (last, far_across)], rows_near[1])
    middle_across = across(middle_sum)
    last_out = to_end(last_sum)
    terms = lax.dot_general(
        after(basis, far),
        wide(delta_embed[0]),
        (((0,), (1,)), ((), ())),
        precision=lax.Precision.HIGH,
        preferred_element_type=jnp.float32,
    ).astype(jnp.bfloat16)
    keep = lax.dynamic_slice_in_dim(terms, side * half_rank, half_rank, 0)
    give = lax.dynamic_slice_in_dim(terms, (1 - side) * half_rank, half_rank, 0)
    (kept,) = add_after([(keep, lax.ppermute(give, "tp", SWAP))], middle_sum)

    def term(place):
        return lax.dynamic_slice_in_dim(kept, block_of(place) * rows, rows, 1)

    terms_out = to_inner(jnp.stack([term(3), term(2), term(1)]))
    rows_inner = [to_inner(low)]
    pieces = dense.split(
        near, last, near_in, middle_across, last_out, rows_far[0], rows_across[1], rows_inner[0]
    )
    rows_inner.append(to_inner(hold(high, pieces)))
    rows_across_2 = [across(part) for part in rows_inner]

    far_terms, middle_terms = add_after([(term(3), terms_out[0]), (term(2), terms_out[1])], pieces)
    terms_middle = across(jnp.stack([far_terms, middle_terms]))

    moved = lax.all_to_all(pieces, "shard", split_axis=0, concat_axis=0, tiled=True)
    rows_across_2[0] = hold(rows_across_2[0], moved)
    rows_last = [to_end(part) for part in rows_across_2]
    next_weights, next_momentum, copies = dense.update(
        moved, owner_weights, owner_momentum, rows_far[1], rows_across_2[0], rows_inner[1]
    )
    (last_terms,) = add_after([(term(0), terms_middle[0])], copies)
    terms_in = to_end(last_terms)
    back = lax.all_to_all(copies, "shard", split_axis=0, concat_axis=0, tiled=True)
    new_block = dense.join(back, rows_last[0], rows_across_2[1])
    block_near = permute(new_block, NEAR)
    block_across = across(new_block)

    mine = jnp.where(end, term(0), term(1))
    sent = mean_after(groups, (mine, terms_out[2], terms_middle[1], terms_in), new_block)
    other = lax.ppermute(sent, "tp", SWAP)

    def both(one, two):
        return jnp.where(side == 0, jnp.concatenate([one, two]), jnp.concatenate([two, one]))

    coefficients = wide(both(sent, other))
    next_embed_momentum = MOMENTUM * embed_momentum[0, 0].T + coefficients
    direction = coefficients + MOMENTUM * next_embed_momentum

    def update(toward, precision):
        return OUTER_RATE * lax.dot_general(
            toward, basis, (((0,), (1,)), ((), ())), precision=precision, preferred_element_type=jnp.float32
        )

    next_embed = embed_owner[0, 0] - update(direction, lax.Precision.HIGHEST)
    half = lax.dynamic_slice_in_dim(direction, side * half_rank, half_rank, 0).astype(jnp.bfloat16)
    half = after(half, block_near, block_across)

    rank = lax.axis_index("rep")
    halves = jnp.stack([permute(half, [(i, (i + step) % groups) for i in range(groups)]) for step in (1, 2, 3)])
    others = lax.ppermute(halves, "tp", SWAP)
    block_far = to_end(block_across)
    block_across_2 = hold(across(block_near), rows_last[1], others)
    block_last = to_end(block_across_2)

    fresh = dense.place(None, 0, new_block, new_block)
    fresh = dense.place(fresh, 1, block_near, block_near)
    fresh = dense.place(fresh, 2, block_far, block_across)
    fresh = dense.place(fresh, 3, block_last, block_across_2)

    fresh_embed = jnp.zeros((groups * rows, embed_owner.shape[3]), jnp.bfloat16)

    def put(target, value, step, start):
        return lax.dynamic_update_slice_in_dim(target, value.astype(target.dtype), block_at(step) * rows + start, 0)

    fresh_embed = put(fresh_embed, next_embed, 0, 0)
    arrived = [(1, rows_near, rows_inner), (2, rows_far, rows_across), (3, rows_last, rows_across_2)]
    for step, at_ends, inside in arrived:
        back_by = (rank - block_at(step) - 1) % groups
        here, there = (lax.dynamic_index_in_dim(part, back_by, 0, False) for part in (halves, others))
        toward = both(here, there)
        for start, one, two in zip((0, cut), at_ends, inside):
            part = jnp.where(end, one, two)
            change = update(wide(toward[:, start : start + part.shape[0]]), lax.Precision.DEFAULT)
            fresh_embed = put(fresh_embed, wide(part) - change, step, start)
    return (
        fresh[0],
        fresh[1],
        fresh[2],
        fresh[3],
        next_weights,
        next_momentum,
        fresh_embed,
        next_embed[None, None],
        next_embed_momentum.T[None, None],
    )


def solution(mesh):
    in_specs = (
        P("rep", None, "shard", "tp"),
        P("rep", None, "shard", "tp"),
        P("rep", None, "shard", "tp"),
        P("rep", None, "shard", "tp"),
        P("rep", "shard", "tp", None),
        P("rep", "shard", "tp", None),
        P("rep", "shard", "tp"),
        P("shard", "rep", None, "tp"),
        P("shard", "rep", None, None),
        P("tp", None),
    )
    out_specs = (
        P(None, "shard", "tp"),
        P(None, "shard", "tp"),
        P(None, "shard", "tp"),
        P(None, "shard", "tp"),
        P("rep", "shard", "tp", None),
        P("rep", "shard", "tp", None),
        P("shard", "tp"),
        P("shard", "rep", None, "tp"),
        P("shard", "rep", None, None),
    )
    return jax.shard_map(local, mesh=mesh, in_specs=in_specs, out_specs=out_specs, check_vma=False)
```

```python
import functools

import jax
import jax.numpy as jnp
from jax import lax
from jax.experimental import pallas as pl
from jax.experimental.pallas import tpu as pltpu
from jax.sharding import PartitionSpec as P

MOMENTUM = 0.5
OUTER_RATE = 0.7
LANES = 128

OUT_IN = [(0, 1), (3, 2)]
MIDDLE = [(1, 2), (2, 1)]
IN_OUT = [(1, 0), (2, 3)]
NEAR = OUT_IN + IN_OUT
SWAP = [(0, 1), (1, 0)]


def permute(value, pairs):
    return lax.ppermute(value, "rep", pairs)


def wide(value):
    return value.astype(jnp.float32)


def add(one, two):
    return (wide(one) + wide(two)).astype(one.dtype)


def at_end():
    rank = lax.axis_index("rep")
    return (rank == 0) | (rank == 3)


def block_of(place):
    return jnp.where(lax.axis_index("rep") >= 2, 3 - place, place)


def block_at(step):
    if step == 0:
        return lax.axis_index("rep")
    return block_of(jnp.where(at_end(), 1, 0)) if step == 1 else block_of(step)


class Kind:
    def __init__(self, delta, groups, shards, sub, width, panel, column):
        self.layers, self.rows, self.cols = delta.shape[1:]
        self.count = self.rows // groups
        self.over = self.count // sub
        self.across = self.cols // width
        self.piece = self.cols // shards
        self.panel = panel
        self.column = column


def make_kinds(deltas, groups, shards):
    width = min(delta.shape[3] for delta in deltas)
    sub = min(delta.shape[2] for delta in deltas) // groups
    kinds = []
    panel = column = 0
    for delta in deltas:
        kind = Kind(delta, groups, shards, sub, width, panel, column)
        kinds.append(kind)
        panel = panel + kind.over * kind.across
        column = column + kind.over * kind.piece
    return kinds, sub, width, panel, column


def each_panel(kinds, sub, width):
    for index, kind in enumerate(kinds):
        for group in range(kind.over):
            for across in range(kind.across):
                panel = kind.panel + group * kind.across + across
                for layer in range(kind.layers):
                    yield index, layer, group * sub, across * width, panel, layer * sub


def pack_kernel(kinds, sub, width, *refs):
    deltas, blocks, sem = refs[: len(kinds)], refs[len(kinds) : -1], refs[-1]
    for order, target in enumerate(blocks):
        block = block_of(len(blocks) - 1 - order)
        for index, layer, row, column, panel, at in each_panel(kinds, sub, width):
            start = pl.multiple_of(block * kinds[index].count + row, 16)
            source = deltas[index].at[0, layer, pl.ds(start, sub), pl.ds(column, width)]
            pltpu.make_async_copy(source, target.at[panel, pl.ds(at, sub), :], sem.at[order]).start()
    for order, target in enumerate(blocks):
        pltpu.make_async_copy(target, target, sem.at[order]).wait()


def place_kernel(kinds, sub, width, step, *refs):
    one, two = refs[:2]
    fresh, sem = refs[-1 - len(kinds) : -1], refs[-1]
    block = block_at(step)

    def start(source):
        for index, layer, row, column, panel, at in each_panel(kinds, sub, width):
            first = pl.multiple_of(block * kinds[index].count + row, 16)
            target = fresh[index].at[layer, pl.ds(first, sub), pl.ds(column, width)]
            pltpu.make_async_copy(source.at[panel, pl.ds(at, sub), :], target, sem).start()

    pl.when(at_end())(lambda: start(one))
    pl.when(jnp.logical_not(at_end()))(lambda: start(two))
    pltpu.make_async_copy(one, one, sem).wait()


def split_kernel(kinds, width, shards, near, last, from_out, from_middle, from_in, *refs):
    end, pieces = at_end(), refs[-1]
    for kind in kinds:
        for group in range(kind.over):
            parts = []
            for across in range(kind.across):
                panel = kind.panel + group * kind.across + across
                mine = jnp.where(end, wide(last[panel]), wide(near[panel]))
                arrived = wide(from_out[panel]) + wide(from_middle[panel]) + wide(from_in[panel])
                parts.append(mine + arrived)
            whole = jnp.concatenate(parts, axis=1)
            column = kind.column + group * kind.piece
            for s in range(shards):
                part = whole[:, s * kind.piece : (s + 1) * kind.piece]
                pieces[s, :, column : column + kind.piece] = part.astype(pieces.dtype)


def join_kernel(kinds, width, shards, pieces, *refs):
    panels = refs[-1]
    wholes = [wide(pieces[s]) for s in range(shards)]
    for kind in kinds:
        for group in range(kind.over):
            column = kind.column + group * kind.piece
            whole = jnp.concatenate([part[:, column : column + kind.piece] for part in wholes], axis=1)
            for across in range(kind.across):
                panel = kind.panel + group * kind.across + across
                panels[panel] = whole[:, across * width : (across + 1) * width].astype(panels.dtype)


def owner_update_kernel(units, shards, groups, moved, weights, momentum, *refs):
    next_weights, next_momentum, back = refs[-3:]
    for flat, row, rows, column, piece in units:
        here = slice(row, row + rows)
        parts = [moved[s, here, :].astype(jnp.float32)[:, column : column + piece] for s in range(shards)]
        gradient = jnp.concatenate(parts, axis=1) / groups
        tiles = shards * piece // LANES
        fresh = []
        for tile in range(tiles):
            at = pl.ds(flat + tile, rows, stride=tiles)
            grad = gradient[:, tile * LANES : (tile + 1) * LANES]
            new_momentum = MOMENTUM * momentum[at, :] + grad
            new_weights = weights[at, :] - OUTER_RATE * (grad + MOMENTUM * new_momentum)
            next_momentum[at, :] = new_momentum
            next_weights[at, :] = new_weights
            fresh.append(new_weights)
        fresh = jnp.concatenate(fresh, axis=1)
        for s in range(shards):
            back[s, here, column : column + piece] = fresh[:, s * piece : (s + 1) * piece].astype(back.dtype)


def kernel_call(body, out_shape, moved_bytes, **more):
    return pl.pallas_call(
        body,
        out_shape=out_shape,
        compiler_params=pltpu.CompilerParams(vmem_limit_bytes=40 << 20),
        cost_estimate=pl.CostEstimate(flops=0, bytes_accessed=moved_bytes, transcendentals=0),
        **more,
    )


ANYWHERE = pl.BlockSpec(memory_space=pl.ANY)
IN_VMEM = pl.BlockSpec(memory_space=pltpu.VMEM)


def copy_kernel(value, *refs):
    refs[-1][...] = value[...]


def after(value, *others):
    return kernel_call(
        copy_kernel,
        jax.ShapeDtypeStruct(value.shape, value.dtype),
        2 * value.size * value.dtype.itemsize,
        in_specs=[IN_VMEM] + [ANYWHERE] * len(others),
    )(value, *others)


def hold_kernel(*refs):
    pass


def hold(value, *others):
    return kernel_call(
        hold_kernel,
        jax.ShapeDtypeStruct(value.shape, value.dtype),
        0,
        in_specs=[ANYWHERE] * (1 + len(others)),
        out_specs=ANYWHERE,
        input_output_aliases={0: 0},
    )(value, *others)


def add_kernel(count, *refs):
    for one, two, total in zip(refs[:count], refs[count : 2 * count], refs[-count:]):
        total[...] = (wide(one[...]) + wide(two[...])).astype(total.dtype)


def add_after(pairs, *others):
    count = len(pairs)
    return kernel_call(
        functools.partial(add_kernel, count),
        [jax.ShapeDtypeStruct(one.shape, one.dtype) for one, _ in pairs],
        6 * sum(one.size for one, _ in pairs),
        in_specs=[IN_VMEM] * (2 * count) + [ANYWHERE] * len(others),
    )(*[one for one, _ in pairs], *[two for _, two in pairs], *others)


def mean_kernel(count, groups, *refs):
    refs[-1][...] = (sum(wide(ref[...]) for ref in refs[:count]) / groups).astype(refs[-1].dtype)


def mean_after(groups, terms, *others):
    return kernel_call(
        functools.partial(mean_kernel, len(terms), groups),
        jax.ShapeDtypeStruct(terms[0].shape, terms[0].dtype),
        10 * terms[0].size,
        in_specs=[IN_VMEM] * len(terms) + [ANYWHERE] * len(others),
    )(*terms, *others)


def narrow_kernel(cut, wide_rows, low, high):
    low[...] = wide_rows[:cut, :].astype(low.dtype)
    high[...] = wide_rows[cut:, :].astype(high.dtype)


def narrow_rows(array, cut):
    rows, columns = array.shape[2:]
    if cut % 16 or rows % 8:
        return [part.astype(jnp.bfloat16) for part in (array[0, 0, :cut], array[0, 0, cut:])]
    return kernel_call(
        functools.partial(narrow_kernel, cut),
        [jax.ShapeDtypeStruct((count, columns), jnp.bfloat16) for count in (cut, rows - cut)],
        6 * rows * columns,
    )(array.reshape(rows, columns))


class Dense:
    def __init__(self, deltas, groups, shards):
        self.groups, self.shards = groups, shards
        self.kinds, self.sub, self.width, self.panels, self.columns = make_kinds(deltas, groups, shards)
        self.layers = deltas[0].shape[1]
        self.dtype = deltas[0].dtype
        self.block_shape = (self.panels, self.layers * self.sub, self.width)
        self.block_bytes = 2 * self.panels * self.layers * self.sub * self.width
        self.aligned = self.sub % 16 == 0 and self.width % LANES == 0
        self.aligned = self.aligned and all(shards * kind.piece % LANES == 0 for kind in self.kinds)

    def pack(self, deltas):
        if self.aligned:
            return kernel_call(
                functools.partial(pack_kernel, self.kinds, self.sub, self.width),
                [jax.ShapeDtypeStruct(self.block_shape, self.dtype)] * 4,
                8 * self.block_bytes,
                in_specs=[ANYWHERE] * len(deltas),
                out_specs=[ANYWHERE] * 4,
                scratch_shapes=[pltpu.SemaphoreType.DMA((4,))],
            )(*deltas)

        def block_panels(block):
            panels = []
            for kind, delta in zip(self.kinds, deltas):
                part = lax.dynamic_slice_in_dim(delta[0], block * kind.count, kind.count, 1)
                part = part.reshape(kind.layers, kind.over, self.sub, kind.across, self.width)
                panels.append(part.transpose(1, 3, 0, 2, 4).reshape(-1, *self.block_shape[1:]))
            return jnp.concatenate(panels)

        return [block_panels(block_of(place)) for place in (3, 2, 1, 0)]

    def as_kinds(self, block):
        parts = []
        for kind in self.kinds:
            part = block[kind.panel : kind.panel + kind.over * kind.across]
            part = part.reshape(kind.over, kind.across, kind.layers, self.sub, self.width)
            parts.append(part.transpose(2, 0, 3, 1, 4).reshape(kind.layers, kind.over, self.sub, kind.cols))
        return parts

    def split(self, near, last, from_out, from_middle, from_in, *others):
        shape = (self.shards, self.layers * self.sub, self.columns)
        if self.aligned:
            return kernel_call(
                functools.partial(split_kernel, self.kinds, self.width, self.shards),
                jax.ShapeDtypeStruct(shape, self.dtype),
                9 * self.block_bytes,
                in_specs=[IN_VMEM] * 5 + [ANYWHERE] * len(others),
            )(near, last, from_out, from_middle, from_in, *others)
        mine = jnp.where(at_end(), last, near)
        total = wide(mine) + wide(from_out) + wide(from_middle) + wide(from_in)
        pieces = []
        for kind, part in zip(self.kinds, self.as_kinds(total.astype(self.dtype))):
            part = part.reshape(kind.layers, kind.over, self.sub, self.shards, kind.piece)
            pieces.append(part.transpose(3, 0, 2, 1, 4).reshape(shape[:2] + (kind.over * kind.piece,)))
        return jnp.concatenate(pieces, axis=2)

    def join(self, pieces, *others):
        if self.aligned:
            return kernel_call(
                functools.partial(join_kernel, self.kinds, self.width, self.shards),
                jax.ShapeDtypeStruct(self.block_shape, self.dtype),
                2 * self.block_bytes,
                in_specs=[IN_VMEM] + [ANYWHERE] * len(others),
            )(pieces, *others)
        panels = []
        for kind in self.kinds:
            part = pieces[..., kind.column : kind.column + kind.over * kind.piece]
            part = part.reshape(self.shards, kind.layers, self.sub, kind.over, kind.piece)
            part = part.transpose(3, 1, 2, 0, 4).reshape(kind.over, kind.layers, self.sub, kind.across, self.width)
            panels.append(part.transpose(0, 3, 1, 2, 4).reshape(-1, *self.block_shape[1:]))
        return jnp.concatenate(panels)

    def place(self, fresh, step, one, two):
        shapes = [(kind.layers, kind.rows, kind.cols) for kind in self.kinds]
        if self.aligned:
            before = fresh or []
            return kernel_call(
                functools.partial(place_kernel, self.kinds, self.sub, self.width, step),
                [jax.ShapeDtypeStruct(shape, self.dtype) for shape in shapes],
                2 * self.block_bytes,
                in_specs=[ANYWHERE] * (2 + len(before)),
                out_specs=[ANYWHERE] * len(shapes),
                scratch_shapes=[pltpu.SemaphoreType.DMA],
                input_output_aliases={2 + index: index for index in range(len(before))},
            )(one, two, *before)
        fresh = fresh or [jnp.zeros(shape, self.dtype) for shape in shapes]
        block = jnp.where(at_end(), one, two)
        placed = []
        for kind, target, part in zip(self.kinds, fresh, self.as_kinds(block)):
            part = part.reshape(kind.layers, kind.count, kind.cols)
            placed.append(lax.dynamic_update_slice_in_dim(target, part, block_at(step) * kind.count, 1))
        return placed

    def update(self, moved, weights, momentum, *others):
        if self.aligned:
            units = []
            flat = 0
            for kind in self.kinds:
                for layer in range(kind.layers):
                    for group in range(kind.over):
                        column = kind.column + group * kind.piece
                        units.append((flat, layer * self.sub, self.sub, column, kind.piece))
                        flat = flat + self.sub * self.shards * kind.piece // LANES
            flat_shape = jax.ShapeDtypeStruct((flat, LANES), jnp.float32)
            next_weights, next_momentum, back = kernel_call(
                functools.partial(owner_update_kernel, units, self.shards, self.groups),
                (flat_shape, flat_shape, jax.ShapeDtypeStruct(moved.shape, moved.dtype)),
                10 * self.block_bytes,
                in_specs=[IN_VMEM] * 3 + [ANYWHERE] * len(others),
            )(moved, weights.reshape(flat, LANES), momentum.reshape(flat, LANES), *others)
            return next_weights.reshape(weights.shape), next_momentum.reshape(weights.shape), back
        flats = []
        for kind in self.kinds:
            part = moved[..., kind.column : kind.column + kind.over * kind.piece]
            part = part.reshape(self.shards, kind.layers, self.sub, kind.over, kind.piece)
            flats.append(part.transpose(1, 3, 2, 0, 4).reshape(-1))
        gradient = (wide(jnp.concatenate(flats)) / self.groups).reshape(weights.shape)
        next_momentum = MOMENTUM * momentum + gradient
        next_weights = weights - OUTER_RATE * (gradient + MOMENTUM * next_momentum)
        copies = next_weights.astype(moved.dtype).reshape(-1)
        returning = []
        at = 0
        for kind in self.kinds:
            count = kind.layers * kind.count * kind.cols
            part = copies[at : at + count].reshape(kind.layers, kind.over, self.sub, self.shards, kind.piece)
            returning.append(part.transpose(3, 0, 2, 1, 4).reshape(moved.shape[:2] + (kind.over * kind.piece,)))
            at = at + count
        return next_weights, next_momentum, jnp.concatenate(returning, axis=2)


def local(
    delta_inputs,
    delta_mixing,
    delta_expand,
    delta_reduce,
    owner_weights,
    owner_momentum,
    delta_embed,
    embed_owner,
    embed_momentum,
    basis,
):
    groups = lax.axis_size("rep")
    shards = lax.axis_size("shard")
    side = lax.axis_index("tp")
    end = at_end()
    deltas = (delta_inputs, delta_mixing, delta_expand, delta_reduce)
    dense = Dense(deltas, groups, shards)


    def to_end(value):
        return permute(value, IN_OUT)

    def across(value):
        return permute(value, MIDDLE)

    def to_inner(value):
        return permute(value, OUT_IN)

    rows = embed_owner.shape[2]
    half_rank = basis.shape[1] // 2
    cut = rows // 2 // LANES * LANES
    low, high = narrow_rows(embed_owner, cut)
    rows_near = [to_end(low), to_end(high)]
    rows_across = [across(low), across(high)]
    rows_far = [to_end(part) for part in rows_across]

    far, middle, near, last = dense.pack(deltas)
    far_in, middle_in, near_in = (to_inner(part) for part in (far, middle, near))
    (far_sum,) = add_after([(far, far_in)], rows_near[0], rows_across[0])
    far_across = across(far_sum)
    middle_sum, last_sum = add_after([(middle, middle_in), (last, far_across)], rows_near[1])
    middle_across = across(middle_sum)
    last_out = to_end(last_sum)
    terms = lax.dot_general(
        after(basis, far),
        wide(delta_embed[0]),
        (((0,), (1,)), ((), ())),
        precision=lax.Precision.HIGH,
        preferred_element_type=jnp.float32,
    ).astype(jnp.bfloat16)
    keep = lax.dynamic_slice_in_dim(terms, side * half_rank, half_rank, 0)
    give = lax.dynamic_slice_in_dim(terms, (1 - side) * half_rank, half_rank, 0)
    (kept,) = add_after([(keep, lax.ppermute(give, "tp", SWAP))], middle_sum)

    def term(place):
        return lax.dynamic_slice_in_dim(kept, block_of(place) * rows, rows, 1)

    terms_out = to_inner(jnp.stack([term(3), term(2), term(1)]))
    rows_inner = [to_inner(low)]
    pieces = dense.split(
        near, last, near_in, middle_across, last_out, rows_far[0], rows_across[1], rows_inner[0]
    )
    rows_inner.append(to_inner(hold(high, pieces)))
    rows_across_2 = [across(part) for part in rows_inner]

    far_terms, middle_terms = add_after([(term(3), terms_out[0]), (term(2), terms_out[1])], pieces)
    terms_middle = across(jnp.stack([far_terms, middle_terms]))

    moved = lax.all_to_all(pieces, "shard", split_axis=0, concat_axis=0, tiled=True)
    rows_across_2[0] = hold(rows_across_2[0], moved)
    rows_last = [to_end(part) for part in rows_across_2]
    next_weights, next_momentum, copies = dense.update(
        moved, owner_weights, owner_momentum, rows_far[1], rows_across_2[0], rows_inner[1]
    )
    (last_terms,) = add_after([(term(0), terms_middle[0])], copies)
    terms_in = to_end(last_terms)
    back = lax.all_to_all(copies, "shard", split_axis=0, concat_axis=0, tiled=True)
    new_block = dense.join(back)
    block_near = permute(new_block, NEAR)
    block_across = across(new_block)

    mine = jnp.where(end, term(0), term(1))
    sent = mean_after(groups, (mine, terms_out[2], terms_middle[1], terms_in), new_block, rows_last[0], rows_across_2[1])
    other = lax.ppermute(sent, "tp", SWAP)

    def both(one, two):
        return jnp.where(side == 0, jnp.concatenate([one, two]), jnp.concatenate([two, one]))

    coefficients = wide(both(sent, other))
    next_embed_momentum = MOMENTUM * embed_momentum[0, 0].T + coefficients
    direction = coefficients + MOMENTUM * next_embed_momentum

    def update(toward, precision):
        return OUTER_RATE * lax.dot_general(
            toward, basis, (((0,), (1,)), ((), ())), precision=precision, preferred_element_type=jnp.float32
        )

    next_embed = embed_owner[0, 0] - update(direction, lax.Precision.HIGHEST)
    half = lax.dynamic_slice_in_dim(direction, side * half_rank, half_rank, 0).astype(jnp.bfloat16)
    half = after(half, block_near)

    rank = lax.axis_index("rep")
    halves = jnp.stack([permute(half, [(i, (i + step) % groups) for i in range(groups)]) for step in (1, 2, 3)])
    others = lax.ppermute(halves, "tp", SWAP)
    block_far = to_end(block_across)
    block_across_2 = hold(across(block_near), rows_last[1], others)
    block_last = to_end(block_across_2)

    fresh = dense.place(None, 0, new_block, new_block)
    fresh = dense.place(fresh, 1, block_near, block_near)
    fresh = dense.place(fresh, 2, block_far, block_across)
    fresh = dense.place(fresh, 3, block_last, block_across_2)

    fresh_embed = jnp.zeros((groups * rows, embed_owner.shape[3]), jnp.bfloat16)

    def put(target, value, step, start):
        return lax.dynamic_update_slice_in_dim(target, value.astype(target.dtype), block_at(step) * rows + start, 0)

    fresh_embed = put(fresh_embed, next_embed, 0, 0)
    arrived = [(1, rows_near, rows_inner), (2, rows_far, rows_across), (3, rows_last, rows_across_2)]
    for step, at_ends, inside in arrived:
        back_by = (rank - block_at(step) - 1) % groups
        here, there = (lax.dynamic_index_in_dim(part, back_by, 0, False) for part in (halves, others))
        toward = both(here, there)
        for start, one, two in zip((0, cut), at_ends, inside):
            part = jnp.where(end, one, two)
            change = update(wide(toward[:, start : start + part.shape[0]]), lax.Precision.DEFAULT)
            fresh_embed = put(fresh_embed, wide(part) - change, step, start)
    return (
        fresh[0],
        fresh[1],
        fresh[2],
        fresh[3],
        next_weights,
        next_momentum,
        fresh_embed,
        next_embed[None, None],
        next_embed_momentum.T[None, None],
    )


def solution(mesh):
    in_specs = (
        P("rep", None, "shard", "tp"),
        P("rep", None, "shard", "tp"),
        P("rep", None, "shard", "tp"),
        P("rep", None, "shard", "tp"),
        P("rep", "shard", "tp", None),
        P("rep", "shard", "tp", None),
        P("rep", "shard", "tp"),
        P("shard", "rep", None, "tp"),
        P("shard", "rep", None, None),
        P("tp", None),
    )
    out_specs = (
        P(None, "shard", "tp"),
        P(None, "shard", "tp"),
        P(None, "shard", "tp"),
        P(None, "shard", "tp"),
        P("rep", "shard", "tp", None),
        P("rep", "shard", "tp", None),
        P("shard", "tp"),
        P("shard", "rep", None, "tp"),
        P("shard", "rep", None, None),
    )
    return jax.shard_map(local, mesh=mesh, in_specs=in_specs, out_specs=out_specs, check_vma=False)
```

```python
import functools

import jax
import jax.numpy as jnp
from jax import lax
from jax.experimental import pallas as pl
from jax.experimental.pallas import tpu as pltpu
from jax.sharding import PartitionSpec as P

MOMENTUM = 0.5
OUTER_RATE = 0.7
LANES = 128

OUT_IN = [(0, 1), (3, 2)]
MIDDLE = [(1, 2), (2, 1)]
IN_OUT = [(1, 0), (2, 3)]
NEAR = OUT_IN + IN_OUT
SWAP = [(0, 1), (1, 0)]


def permute(value, pairs):
    return lax.ppermute(value, "rep", pairs)


def wide(value):
    return value.astype(jnp.float32)


def add(one, two):
    return (wide(one) + wide(two)).astype(one.dtype)


def at_end():
    rank = lax.axis_index("rep")
    return (rank == 0) | (rank == 3)


def block_of(place):
    return jnp.where(lax.axis_index("rep") >= 2, 3 - place, place)


def block_at(step):
    if step == 0:
        return lax.axis_index("rep")
    return block_of(jnp.where(at_end(), 1, 0)) if step == 1 else block_of(step)


class Kind:
    def __init__(self, delta, groups, shards, sub, width, panel, column):
        self.layers, self.rows, self.cols = delta.shape[1:]
        self.count = self.rows // groups
        self.over = self.count // sub
        self.across = self.cols // width
        self.piece = self.cols // shards
        self.panel = panel
        self.column = column


def make_kinds(deltas, groups, shards):
    width = min(delta.shape[3] for delta in deltas)
    sub = min(delta.shape[2] for delta in deltas) // groups
    kinds = []
    panel = column = 0
    for delta in deltas:
        kind = Kind(delta, groups, shards, sub, width, panel, column)
        kinds.append(kind)
        panel = panel + kind.over * kind.across
        column = column + kind.over * kind.piece
    return kinds, sub, width, panel, column


def each_panel(kinds, sub, width):
    for index, kind in enumerate(kinds):
        for group in range(kind.over):
            for across in range(kind.across):
                panel = kind.panel + group * kind.across + across
                for layer in range(kind.layers):
                    yield index, layer, group * sub, across * width, panel, layer * sub


def pack_kernel(kinds, sub, width, *refs):
    deltas, blocks, sem = refs[: len(kinds)], refs[len(kinds) : -1], refs[-1]
    for order, target in enumerate(blocks):
        block = block_of(len(blocks) - 1 - order)
        for index, layer, row, column, panel, at in each_panel(kinds, sub, width):
            start = pl.multiple_of(block * kinds[index].count + row, 16)
            source = deltas[index].at[0, layer, pl.ds(start, sub), pl.ds(column, width)]
            pltpu.make_async_copy(source, target.at[panel, pl.ds(at, sub), :], sem.at[order]).start()
    for order, target in enumerate(blocks):
        pltpu.make_async_copy(target, target, sem.at[order]).wait()


def place_kernel(kinds, sub, width, step, *refs):
    one, two = refs[:2]
    fresh, sem = refs[-1 - len(kinds) : -1], refs[-1]
    block = block_at(step)

    def start(source):
        for index, layer, row, column, panel, at in each_panel(kinds, sub, width):
            first = pl.multiple_of(block * kinds[index].count + row, 16)
            target = fresh[index].at[layer, pl.ds(first, sub), pl.ds(column, width)]
            pltpu.make_async_copy(source.at[panel, pl.ds(at, sub), :], target, sem).start()

    pl.when(at_end())(lambda: start(one))
    pl.when(jnp.logical_not(at_end()))(lambda: start(two))
    pltpu.make_async_copy(one, one, sem).wait()


def split_kernel(kinds, width, shards, near, last, from_out, from_middle, from_in, *refs):
    end, pieces = at_end(), refs[-1]
    for kind in kinds:
        for group in range(kind.over):
            parts = []
            for across in range(kind.across):
                panel = kind.panel + group * kind.across + across
                mine = jnp.where(end, wide(last[panel]), wide(near[panel]))
                arrived = wide(from_out[panel]) + wide(from_middle[panel]) + wide(from_in[panel])
                parts.append(mine + arrived)
            whole = jnp.concatenate(parts, axis=1)
            column = kind.column + group * kind.piece
            for s in range(shards):
                part = whole[:, s * kind.piece : (s + 1) * kind.piece]
                pieces[s, :, column : column + kind.piece] = part.astype(pieces.dtype)


def join_kernel(kinds, width, shards, pieces, *refs):
    panels = refs[-1]
    wholes = [wide(pieces[s]) for s in range(shards)]
    for kind in kinds:
        for group in range(kind.over):
            column = kind.column + group * kind.piece
            whole = jnp.concatenate([part[:, column : column + kind.piece] for part in wholes], axis=1)
            for across in range(kind.across):
                panel = kind.panel + group * kind.across + across
                panels[panel] = whole[:, across * width : (across + 1) * width].astype(panels.dtype)


def owner_update_kernel(units, shards, groups, moved, weights, momentum, *refs):
    next_weights, next_momentum, back = refs[-3:]
    for flat, row, rows, column, piece in units:
        here = slice(row, row + rows)
        parts = [moved[s, here, :].astype(jnp.float32)[:, column : column + piece] for s in range(shards)]
        gradient = jnp.concatenate(parts, axis=1) / groups
        tiles = shards * piece // LANES
        fresh = []
        for tile in range(tiles):
            at = pl.ds(flat + tile, rows, stride=tiles)
            grad = gradient[:, tile * LANES : (tile + 1) * LANES]
            new_momentum = MOMENTUM * momentum[at, :] + grad
            new_weights = weights[at, :] - OUTER_RATE * (grad + MOMENTUM * new_momentum)
            next_momentum[at, :] = new_momentum
            next_weights[at, :] = new_weights
            fresh.append(new_weights)
        fresh = jnp.concatenate(fresh, axis=1)
        for s in range(shards):
            back[s, here, column : column + piece] = fresh[:, s * piece : (s + 1) * piece].astype(back.dtype)


def kernel_call(body, out_shape, moved_bytes, vmem=40, **more):
    return pl.pallas_call(
        body,
        out_shape=out_shape,
        compiler_params=pltpu.CompilerParams(vmem_limit_bytes=vmem << 20),
        cost_estimate=pl.CostEstimate(flops=0, bytes_accessed=moved_bytes, transcendentals=0),
        **more,
    )


ANYWHERE = pl.BlockSpec(memory_space=pl.ANY)
IN_VMEM = pl.BlockSpec(memory_space=pltpu.VMEM)


def copy_kernel(value, *refs):
    refs[-1][...] = value[...]


def after(value, *others):
    return kernel_call(
        copy_kernel,
        jax.ShapeDtypeStruct(value.shape, value.dtype),
        2 * value.size * value.dtype.itemsize,
        in_specs=[IN_VMEM] + [ANYWHERE] * len(others),
    )(value, *others)


def hold_kernel(*refs):
    pass


def hold(value, *others):
    return kernel_call(
        hold_kernel,
        jax.ShapeDtypeStruct(value.shape, value.dtype),
        0,
        in_specs=[ANYWHERE] * (1 + len(others)),
        out_specs=ANYWHERE,
        input_output_aliases={0: 0},
    )(value, *others)


def add_kernel(count, *refs):
    for one, two, total in zip(refs[:count], refs[count : 2 * count], refs[-count:]):
        total[...] = (wide(one[...]) + wide(two[...])).astype(total.dtype)


def add_after(pairs, *others):
    count = len(pairs)
    return kernel_call(
        functools.partial(add_kernel, count),
        [jax.ShapeDtypeStruct(one.shape, one.dtype) for one, _ in pairs],
        6 * sum(one.size for one, _ in pairs),
        in_specs=[IN_VMEM] * (2 * count) + [ANYWHERE] * len(others),
    )(*[one for one, _ in pairs], *[two for _, two in pairs], *others)


def mean_kernel(count, groups, *refs):
    refs[-1][...] = (sum(wide(ref[...]) for ref in refs[:count]) / groups).astype(refs[-1].dtype)


def mean_after(groups, terms, *others):
    return kernel_call(
        functools.partial(mean_kernel, len(terms), groups),
        jax.ShapeDtypeStruct(terms[0].shape, terms[0].dtype),
        10 * terms[0].size,
        in_specs=[IN_VMEM] * len(terms) + [ANYWHERE] * len(others),
    )(*terms, *others)


def narrow_kernel(first, wide_rows, part, held, sem):
    copy = pltpu.make_async_copy(wide_rows.at[pl.ds(first, part.shape[0]), :], held, sem)
    copy.start()
    copy.wait()
    part[...] = held[...].astype(part.dtype)


def narrow_rows(array, first, count):
    rows, columns = array.shape[2:]
    if first % 8 or count % 8:
        return array[0, 0, first : first + count].astype(jnp.bfloat16)
    return kernel_call(
        functools.partial(narrow_kernel, first),
        jax.ShapeDtypeStruct((count, columns), jnp.bfloat16),
        6 * count * columns,
        vmem=60,
        in_specs=[ANYWHERE],
        scratch_shapes=[pltpu.VMEM((count, columns), array.dtype), pltpu.SemaphoreType.DMA],
    )(array.reshape(rows, columns))


class Dense:
    def __init__(self, deltas, groups, shards):
        self.groups, self.shards = groups, shards
        self.kinds, self.sub, self.width, self.panels, self.columns = make_kinds(deltas, groups, shards)
        self.layers = deltas[0].shape[1]
        self.dtype = deltas[0].dtype
        self.block_shape = (self.panels, self.layers * self.sub, self.width)
        self.block_bytes = 2 * self.panels * self.layers * self.sub * self.width
        self.aligned = self.sub % 16 == 0 and self.width % LANES == 0
        self.aligned = self.aligned and all(shards * kind.piece % LANES == 0 for kind in self.kinds)

    def pack(self, deltas):
        if self.aligned:
            return kernel_call(
                functools.partial(pack_kernel, self.kinds, self.sub, self.width),
                [jax.ShapeDtypeStruct(self.block_shape, self.dtype)] * 4,
                8 * self.block_bytes,
                in_specs=[ANYWHERE] * len(deltas),
                out_specs=[ANYWHERE] * 4,
                scratch_shapes=[pltpu.SemaphoreType.DMA((4,))],
            )(*deltas)

        def block_panels(block):
            panels = []
            for kind, delta in zip(self.kinds, deltas):
                part = lax.dynamic_slice_in_dim(delta[0], block * kind.count, kind.count, 1)
                part = part.reshape(kind.layers, kind.over, self.sub, kind.across, self.width)
                panels.append(part.transpose(1, 3, 0, 2, 4).reshape(-1, *self.block_shape[1:]))
            return jnp.concatenate(panels)

        return [block_panels(block_of(place)) for place in (3, 2, 1, 0)]

    def as_kinds(self, block):
        parts = []
        for kind in self.kinds:
            part = block[kind.panel : kind.panel + kind.over * kind.across]
            part = part.reshape(kind.over, kind.across, kind.layers, self.sub, self.width)
            parts.append(part.transpose(2, 0, 3, 1, 4).reshape(kind.layers, kind.over, self.sub, kind.cols))
        return parts

    def split(self, near, last, from_out, from_middle, from_in, *others):
        shape = (self.shards, self.layers * self.sub, self.columns)
        if self.aligned:
            return kernel_call(
                functools.partial(split_kernel, self.kinds, self.width, self.shards),
                jax.ShapeDtypeStruct(shape, self.dtype),
                9 * self.block_bytes,
                in_specs=[IN_VMEM] * 5 + [ANYWHERE] * len(others),
            )(near, last, from_out, from_middle, from_in, *others)
        mine = jnp.where(at_end(), last, near)
        total = wide(mine) + wide(from_out) + wide(from_middle) + wide(from_in)
        pieces = []
        for kind, part in zip(self.kinds, self.as_kinds(total.astype(self.dtype))):
            part = part.reshape(kind.layers, kind.over, self.sub, self.shards, kind.piece)
            pieces.append(part.transpose(3, 0, 2, 1, 4).reshape(shape[:2] + (kind.over * kind.piece,)))
        return jnp.concatenate(pieces, axis=2)

    def join(self, pieces, *others):
        if self.aligned:
            return kernel_call(
                functools.partial(join_kernel, self.kinds, self.width, self.shards),
                jax.ShapeDtypeStruct(self.block_shape, self.dtype),
                2 * self.block_bytes,
                in_specs=[IN_VMEM] + [ANYWHERE] * len(others),
            )(pieces, *others)
        panels = []
        for kind in self.kinds:
            part = pieces[..., kind.column : kind.column + kind.over * kind.piece]
            part = part.reshape(self.shards, kind.layers, self.sub, kind.over, kind.piece)
            part = part.transpose(3, 1, 2, 0, 4).reshape(kind.over, kind.layers, self.sub, kind.across, self.width)
            panels.append(part.transpose(0, 3, 1, 2, 4).reshape(-1, *self.block_shape[1:]))
        return jnp.concatenate(panels)

    def place(self, fresh, step, one, two):
        shapes = [(kind.layers, kind.rows, kind.cols) for kind in self.kinds]
        if self.aligned:
            before = fresh or []
            return kernel_call(
                functools.partial(place_kernel, self.kinds, self.sub, self.width, step),
                [jax.ShapeDtypeStruct(shape, self.dtype) for shape in shapes],
                2 * self.block_bytes,
                in_specs=[ANYWHERE] * (2 + len(before)),
                out_specs=[ANYWHERE] * len(shapes),
                scratch_shapes=[pltpu.SemaphoreType.DMA],
                input_output_aliases={2 + index: index for index in range(len(before))},
            )(one, two, *before)
        fresh = fresh or [jnp.zeros(shape, self.dtype) for shape in shapes]
        block = jnp.where(at_end(), one, two)
        placed = []
        for kind, target, part in zip(self.kinds, fresh, self.as_kinds(block)):
            part = part.reshape(kind.layers, kind.count, kind.cols)
            placed.append(lax.dynamic_update_slice_in_dim(target, part, block_at(step) * kind.count, 1))
        return placed

    def update(self, moved, weights, momentum, *others):
        if self.aligned:
            units = []
            flat = 0
            for kind in self.kinds:
                for layer in range(kind.layers):
                    for group in range(kind.over):
                        column = kind.column + group * kind.piece
                        units.append((flat, layer * self.sub, self.sub, column, kind.piece))
                        flat = flat + self.sub * self.shards * kind.piece // LANES
            flat_shape = jax.ShapeDtypeStruct((flat, LANES), jnp.float32)
            next_weights, next_momentum, back = kernel_call(
                functools.partial(owner_update_kernel, units, self.shards, self.groups),
                (flat_shape, flat_shape, jax.ShapeDtypeStruct(moved.shape, moved.dtype)),
                10 * self.block_bytes,
                in_specs=[IN_VMEM] * 3 + [ANYWHERE] * len(others),
            )(moved, weights.reshape(flat, LANES), momentum.reshape(flat, LANES), *others)
            return next_weights.reshape(weights.shape), next_momentum.reshape(weights.shape), back
        flats = []
        for kind in self.kinds:
            part = moved[..., kind.column : kind.column + kind.over * kind.piece]
            part = part.reshape(self.shards, kind.layers, self.sub, kind.over, kind.piece)
            flats.append(part.transpose(1, 3, 2, 0, 4).reshape(-1))
        gradient = (wide(jnp.concatenate(flats)) / self.groups).reshape(weights.shape)
        next_momentum = MOMENTUM * momentum + gradient
        next_weights = weights - OUTER_RATE * (gradient + MOMENTUM * next_momentum)
        copies = next_weights.astype(moved.dtype).reshape(-1)
        returning = []
        at = 0
        for kind in self.kinds:
            count = kind.layers * kind.count * kind.cols
            part = copies[at : at + count].reshape(kind.layers, kind.over, self.sub, self.shards, kind.piece)
            returning.append(part.transpose(3, 0, 2, 1, 4).reshape(moved.shape[:2] + (kind.over * kind.piece,)))
            at = at + count
        return next_weights, next_momentum, jnp.concatenate(returning, axis=2)


def local(
    delta_inputs,
    delta_mixing,
    delta_expand,
    delta_reduce,
    owner_weights,
    owner_momentum,
    delta_embed,
    embed_owner,
    embed_momentum,
    basis,
):
    groups = lax.axis_size("rep")
    shards = lax.axis_size("shard")
    side = lax.axis_index("tp")
    end = at_end()
    deltas = (delta_inputs, delta_mixing, delta_expand, delta_reduce)
    dense = Dense(deltas, groups, shards)


    def to_end(value):
        return permute(value, IN_OUT)

    def across(value):
        return permute(value, MIDDLE)

    def to_inner(value):
        return permute(value, OUT_IN)

    rows = embed_owner.shape[2]
    half_rank = basis.shape[1] // 2
    cut = rows // 2 // LANES * LANES
    low, high = narrow_rows(embed_owner, 0, cut), narrow_rows(embed_owner, cut, rows - cut)
    rows_near = [to_end(low), to_end(high)]
    rows_across = [across(low), across(high)]
    rows_far = [to_end(part) for part in rows_across]

    far, middle, near, last = dense.pack(deltas)
    far_in, middle_in, near_in = (to_inner(part) for part in (far, middle, near))
    (far_sum,) = add_after([(far, far_in)], rows_near[0], rows_across[0])
    far_across = across(far_sum)
    middle_sum, last_sum = add_after([(middle, middle_in), (last, far_across)], rows_near[1])
    middle_across = across(middle_sum)
    last_out = to_end(last_sum)
    terms = lax.dot_general(
        after(basis, far),
        wide(delta_embed[0]),
        (((0,), (1,)), ((), ())),
        precision=lax.Precision.HIGH,
        preferred_element_type=jnp.float32,
    ).astype(jnp.bfloat16)
    keep = lax.dynamic_slice_in_dim(terms, side * half_rank, half_rank, 0)
    give = lax.dynamic_slice_in_dim(terms, (1 - side) * half_rank, half_rank, 0)
    (kept,) = add_after([(keep, lax.ppermute(give, "tp", SWAP))], middle_sum)

    def term(place):
        return lax.dynamic_slice_in_dim(kept, block_of(place) * rows, rows, 1)

    terms_out = to_inner(jnp.stack([term(3), term(2), term(1)]))
    rows_inner = [to_inner(low)]
    pieces = dense.split(
        near, last, near_in, middle_across, last_out, rows_far[0], rows_across[1], rows_inner[0]
    )
    rows_inner.append(to_inner(hold(high, pieces)))
    rows_across_2 = [across(part) for part in rows_inner]

    far_terms, middle_terms = add_after([(term(3), terms_out[0]), (term(2), terms_out[1])], pieces)
    terms_middle = across(jnp.stack([far_terms, middle_terms]))

    moved = lax.all_to_all(pieces, "shard", split_axis=0, concat_axis=0, tiled=True)
    rows_across_2[0] = hold(rows_across_2[0], moved)
    rows_last = [to_end(part) for part in rows_across_2]
    next_weights, next_momentum, copies = dense.update(
        moved, owner_weights, owner_momentum, rows_far[1], rows_across_2[0], rows_inner[1]
    )
    (last_terms,) = add_after([(term(0), terms_middle[0])], copies)
    terms_in = to_end(last_terms)
    back = lax.all_to_all(copies, "shard", split_axis=0, concat_axis=0, tiled=True)
    new_block = dense.join(back)
    block_near = permute(new_block, NEAR)
    block_across = across(new_block)

    mine = jnp.where(end, term(0), term(1))
    sent = mean_after(groups, (mine, terms_out[2], terms_middle[1], terms_in), new_block, rows_last[0], rows_across_2[1])
    other = lax.ppermute(sent, "tp", SWAP)

    def both(one, two):
        return jnp.where(side == 0, jnp.concatenate([one, two]), jnp.concatenate([two, one]))

    coefficients = wide(both(sent, other))
    next_embed_momentum = MOMENTUM * embed_momentum[0, 0].T + coefficients
    direction = coefficients + MOMENTUM * next_embed_momentum

    def update(toward, precision):
        return OUTER_RATE * lax.dot_general(
            toward, basis, (((0,), (1,)), ((), ())), precision=precision, preferred_element_type=jnp.float32
        )

    next_embed = embed_owner[0, 0] - update(direction, lax.Precision.HIGHEST)
    half = lax.dynamic_slice_in_dim(direction, side * half_rank, half_rank, 0).astype(jnp.bfloat16)
    half = after(half, block_near)

    rank = lax.axis_index("rep")
    halves = jnp.stack([permute(half, [(i, (i + step) % groups) for i in range(groups)]) for step in (1, 2, 3)])
    others = lax.ppermute(halves, "tp", SWAP)
    block_far = to_end(block_across)
    block_across_2 = hold(across(block_near), rows_last[1], others)
    block_last = to_end(block_across_2)

    fresh = dense.place(None, 0, new_block, new_block)
    fresh = dense.place(fresh, 1, block_near, block_near)
    fresh = dense.place(fresh, 2, block_far, block_across)
    fresh = dense.place(fresh, 3, block_last, block_across_2)

    fresh_embed = jnp.zeros((groups * rows, embed_owner.shape[3]), jnp.bfloat16)

    def put(target, value, step, start):
        return lax.dynamic_update_slice_in_dim(target, value.astype(target.dtype), block_at(step) * rows + start, 0)

    fresh_embed = put(fresh_embed, next_embed, 0, 0)
    arrived = [(1, rows_near, rows_inner), (2, rows_far, rows_across), (3, rows_last, rows_across_2)]
    for step, at_ends, inside in arrived:
        back_by = (rank - block_at(step) - 1) % groups
        here, there = (lax.dynamic_index_in_dim(part, back_by, 0, False) for part in (halves, others))
        toward = both(here, there)
        for start, one, two in zip((0, cut), at_ends, inside):
            part = jnp.where(end, one, two)
            change = update(wide(toward[:, start : start + part.shape[0]]), lax.Precision.DEFAULT)
            fresh_embed = put(fresh_embed, wide(part) - change, step, start)
    return (
        fresh[0],
        fresh[1],
        fresh[2],
        fresh[3],
        next_weights,
        next_momentum,
        fresh_embed,
        next_embed[None, None],
        next_embed_momentum.T[None, None],
    )


def solution(mesh):
    in_specs = (
        P("rep", None, "shard", "tp"),
        P("rep", None, "shard", "tp"),
        P("rep", None, "shard", "tp"),
        P("rep", None, "shard", "tp"),
        P("rep", "shard", "tp", None),
        P("rep", "shard", "tp", None),
        P("rep", "shard", "tp"),
        P("shard", "rep", None, "tp"),
        P("shard", "rep", None, None),
        P("tp", None),
    )
    out_specs = (
        P(None, "shard", "tp"),
        P(None, "shard", "tp"),
        P(None, "shard", "tp"),
        P(None, "shard", "tp"),
        P("rep", "shard", "tp", None),
        P("rep", "shard", "tp", None),
        P("shard", "tp"),
        P("shard", "rep", None, "tp"),
        P("shard", "rep", None, None),
    )
    return jax.shard_map(local, mesh=mesh, in_specs=in_specs, out_specs=out_specs, check_vma=False)
```

```python
import functools

import jax
import jax.numpy as jnp
from jax import lax
from jax.experimental import pallas as pl
from jax.experimental.pallas import tpu as pltpu
from jax.sharding import PartitionSpec as P

MOMENTUM = 0.5
OUTER_RATE = 0.7
LANES = 128

OUT_IN = [(0, 1), (3, 2)]
MIDDLE = [(1, 2), (2, 1)]
IN_OUT = [(1, 0), (2, 3)]
NEAR = OUT_IN + IN_OUT
SWAP = [(0, 1), (1, 0)]


def permute(value, pairs):
    return lax.ppermute(value, "rep", pairs)


def wide(value):
    return value.astype(jnp.float32)


def add(one, two):
    return (wide(one) + wide(two)).astype(one.dtype)


def at_end():
    rank = lax.axis_index("rep")
    return (rank == 0) | (rank == 3)


def block_of(place):
    return jnp.where(lax.axis_index("rep") >= 2, 3 - place, place)


def block_at(step):
    if step == 0:
        return lax.axis_index("rep")
    return block_of(jnp.where(at_end(), 1, 0)) if step == 1 else block_of(step)


class Kind:
    def __init__(self, delta, groups, shards, sub, width, panel, column):
        self.layers, self.rows, self.cols = delta.shape[1:]
        self.count = self.rows // groups
        self.over = self.count // sub
        self.across = self.cols // width
        self.piece = self.cols // shards
        self.panel = panel
        self.column = column


def make_kinds(deltas, groups, shards):
    width = min(delta.shape[3] for delta in deltas)
    sub = min(delta.shape[2] for delta in deltas) // groups
    kinds = []
    panel = column = 0
    for delta in deltas:
        kind = Kind(delta, groups, shards, sub, width, panel, column)
        kinds.append(kind)
        panel = panel + kind.over * kind.across
        column = column + kind.over * kind.piece
    return kinds, sub, width, panel, column


def each_panel(kinds, sub, width):
    for index, kind in enumerate(kinds):
        for group in range(kind.over):
            for across in range(kind.across):
                panel = kind.panel + group * kind.across + across
                for layer in range(kind.layers):
                    yield index, layer, group * sub, across * width, panel, layer * sub


def pack_kernel(kinds, sub, width, *refs):
    deltas, blocks, sem = refs[: len(kinds)], refs[len(kinds) : -1], refs[-1]
    for order, target in enumerate(blocks):
        block = block_of(len(blocks) - 1 - order)
        for index, layer, row, column, panel, at in each_panel(kinds, sub, width):
            start = pl.multiple_of(block * kinds[index].count + row, 16)
            source = deltas[index].at[0, layer, pl.ds(start, sub), pl.ds(column, width)]
            pltpu.make_async_copy(source, target.at[panel, pl.ds(at, sub), :], sem.at[order]).start()
    for order, target in enumerate(blocks):
        pltpu.make_async_copy(target, target, sem.at[order]).wait()


def place_kernel(kinds, sub, width, step, *refs):
    one, two = refs[:2]
    fresh, sem = refs[-1 - len(kinds) : -1], refs[-1]
    block = block_at(step)

    def start(source):
        for index, layer, row, column, panel, at in each_panel(kinds, sub, width):
            first = pl.multiple_of(block * kinds[index].count + row, 16)
            target = fresh[index].at[layer, pl.ds(first, sub), pl.ds(column, width)]
            pltpu.make_async_copy(source.at[panel, pl.ds(at, sub), :], target, sem).start()

    pl.when(at_end())(lambda: start(one))
    pl.when(jnp.logical_not(at_end()))(lambda: start(two))
    pltpu.make_async_copy(one, one, sem).wait()


def split_kernel(kinds, width, shards, near, last, from_out, from_middle, from_in, *refs):
    end, pieces = at_end(), refs[-1]
    for kind in kinds:
        for group in range(kind.over):
            parts = []
            for across in range(kind.across):
                panel = kind.panel + group * kind.across + across
                mine = jnp.where(end, wide(last[panel]), wide(near[panel]))
                arrived = wide(from_out[panel]) + wide(from_middle[panel]) + wide(from_in[panel])
                parts.append(mine + arrived)
            whole = jnp.concatenate(parts, axis=1)
            column = kind.column + group * kind.piece
            for s in range(shards):
                part = whole[:, s * kind.piece : (s + 1) * kind.piece]
                pieces[s, :, column : column + kind.piece] = part.astype(pieces.dtype)


def join_kernel(kinds, width, shards, pieces, *refs):
    panels = refs[-1]
    wholes = [wide(pieces[s]) for s in range(shards)]
    for kind in kinds:
        for group in range(kind.over):
            column = kind.column + group * kind.piece
            whole = jnp.concatenate([part[:, column : column + kind.piece] for part in wholes], axis=1)
            for across in range(kind.across):
                panel = kind.panel + group * kind.across + across
                panels[panel] = whole[:, across * width : (across + 1) * width].astype(panels.dtype)


def owner_update_kernel(units, shards, groups, moved, weights, momentum, *refs):
    next_weights, next_momentum, back = refs[-3:]
    for flat, row, rows, column, piece in units:
        here = slice(row, row + rows)
        parts = [moved[s, here, :].astype(jnp.float32)[:, column : column + piece] for s in range(shards)]
        gradient = jnp.concatenate(parts, axis=1) / groups
        tiles = shards * piece // LANES
        fresh = []
        for tile in range(tiles):
            at = pl.ds(flat + tile, rows, stride=tiles)
            grad = gradient[:, tile * LANES : (tile + 1) * LANES]
            new_momentum = MOMENTUM * momentum[at, :] + grad
            new_weights = weights[at, :] - OUTER_RATE * (grad + MOMENTUM * new_momentum)
            next_momentum[at, :] = new_momentum
            next_weights[at, :] = new_weights
            fresh.append(new_weights)
        fresh = jnp.concatenate(fresh, axis=1)
        for s in range(shards):
            back[s, here, column : column + piece] = fresh[:, s * piece : (s + 1) * piece].astype(back.dtype)


def kernel_call(body, out_shape, moved_bytes, vmem=40, **more):
    return pl.pallas_call(
        body,
        out_shape=out_shape,
        compiler_params=pltpu.CompilerParams(vmem_limit_bytes=vmem << 20),
        cost_estimate=pl.CostEstimate(flops=0, bytes_accessed=moved_bytes, transcendentals=0),
        **more,
    )


ANYWHERE = pl.BlockSpec(memory_space=pl.ANY)
IN_VMEM = pl.BlockSpec(memory_space=pltpu.VMEM)


def copy_kernel(value, *refs):
    refs[-1][...] = value[...]


def after(value, *others):
    return kernel_call(
        copy_kernel,
        jax.ShapeDtypeStruct(value.shape, value.dtype),
        2 * value.size * value.dtype.itemsize,
        in_specs=[IN_VMEM] + [ANYWHERE] * len(others),
    )(value, *others)


def hold_kernel(*refs):
    pass


def hold(value, *others):
    return kernel_call(
        hold_kernel,
        jax.ShapeDtypeStruct(value.shape, value.dtype),
        0,
        in_specs=[ANYWHERE] * (1 + len(others)),
        out_specs=ANYWHERE,
        input_output_aliases={0: 0},
    )(value, *others)


def add_kernel(count, *refs):
    for one, two, total in zip(refs[:count], refs[count : 2 * count], refs[-count:]):
        total[...] = (wide(one[...]) + wide(two[...])).astype(total.dtype)


def add_after(pairs, *others):
    count = len(pairs)
    return kernel_call(
        functools.partial(add_kernel, count),
        [jax.ShapeDtypeStruct(one.shape, one.dtype) for one, _ in pairs],
        6 * sum(one.size for one, _ in pairs),
        in_specs=[IN_VMEM] * (2 * count) + [ANYWHERE] * len(others),
    )(*[one for one, _ in pairs], *[two for _, two in pairs], *others)


def mean_kernel(count, groups, *refs):
    refs[-1][...] = (sum(wide(ref[...]) for ref in refs[:count]) / groups).astype(refs[-1].dtype)


def mean_after(groups, terms, *others):
    return kernel_call(
        functools.partial(mean_kernel, len(terms), groups),
        jax.ShapeDtypeStruct(terms[0].shape, terms[0].dtype),
        10 * terms[0].size,
        in_specs=[IN_VMEM] * len(terms) + [ANYWHERE] * len(others),
    )(*terms, *others)


def narrow_kernel(first, wide_rows, part, held, sem):
    copy = pltpu.make_async_copy(wide_rows.at[pl.ds(first, part.shape[0]), :], held, sem)
    copy.start()
    copy.wait()
    part[...] = held[...].astype(part.dtype)


def narrow_rows(array, first, count):
    rows, columns = array.shape[2:]
    if first % 8 or count % 8:
        return array[0, 0, first : first + count].astype(jnp.bfloat16)
    return kernel_call(
        functools.partial(narrow_kernel, first),
        jax.ShapeDtypeStruct((count, columns), jnp.bfloat16),
        6 * count * columns,
        vmem=60,
        in_specs=[ANYWHERE],
        scratch_shapes=[pltpu.VMEM((count, columns), array.dtype), pltpu.SemaphoreType.DMA],
    )(array.reshape(rows, columns))


class Dense:
    def __init__(self, deltas, groups, shards):
        self.groups, self.shards = groups, shards
        self.kinds, self.sub, self.width, self.panels, self.columns = make_kinds(deltas, groups, shards)
        self.layers = deltas[0].shape[1]
        self.dtype = deltas[0].dtype
        self.block_shape = (self.panels, self.layers * self.sub, self.width)
        self.block_bytes = 2 * self.panels * self.layers * self.sub * self.width
        self.aligned = self.sub % 16 == 0 and self.width % LANES == 0
        self.aligned = self.aligned and all(shards * kind.piece % LANES == 0 for kind in self.kinds)

    def pack(self, deltas):
        if self.aligned:
            return kernel_call(
                functools.partial(pack_kernel, self.kinds, self.sub, self.width),
                [jax.ShapeDtypeStruct(self.block_shape, self.dtype)] * 4,
                8 * self.block_bytes,
                in_specs=[ANYWHERE] * len(deltas),
                out_specs=[ANYWHERE] * 4,
                scratch_shapes=[pltpu.SemaphoreType.DMA((4,))],
            )(*deltas)

        def block_panels(block):
            panels = []
            for kind, delta in zip(self.kinds, deltas):
                part = lax.dynamic_slice_in_dim(delta[0], block * kind.count, kind.count, 1)
                part = part.reshape(kind.layers, kind.over, self.sub, kind.across, self.width)
                panels.append(part.transpose(1, 3, 0, 2, 4).reshape(-1, *self.block_shape[1:]))
            return jnp.concatenate(panels)

        return [block_panels(block_of(place)) for place in (3, 2, 1, 0)]

    def as_kinds(self, block):
        parts = []
        for kind in self.kinds:
            part = block[kind.panel : kind.panel + kind.over * kind.across]
            part = part.reshape(kind.over, kind.across, kind.layers, self.sub, self.width)
            parts.append(part.transpose(2, 0, 3, 1, 4).reshape(kind.layers, kind.over, self.sub, kind.cols))
        return parts

    def split(self, near, last, from_out, from_middle, from_in, *others):
        shape = (self.shards, self.layers * self.sub, self.columns)
        if self.aligned:
            return kernel_call(
                functools.partial(split_kernel, self.kinds, self.width, self.shards),
                jax.ShapeDtypeStruct(shape, self.dtype),
                9 * self.block_bytes,
                in_specs=[IN_VMEM] * 5 + [ANYWHERE] * len(others),
            )(near, last, from_out, from_middle, from_in, *others)
        mine = jnp.where(at_end(), last, near)
        total = wide(mine) + wide(from_out) + wide(from_middle) + wide(from_in)
        pieces = []
        for kind, part in zip(self.kinds, self.as_kinds(total.astype(self.dtype))):
            part = part.reshape(kind.layers, kind.over, self.sub, self.shards, kind.piece)
            pieces.append(part.transpose(3, 0, 2, 1, 4).reshape(shape[:2] + (kind.over * kind.piece,)))
        return jnp.concatenate(pieces, axis=2)

    def join(self, pieces, *others):
        if self.aligned:
            return kernel_call(
                functools.partial(join_kernel, self.kinds, self.width, self.shards),
                jax.ShapeDtypeStruct(self.block_shape, self.dtype),
                2 * self.block_bytes,
                in_specs=[IN_VMEM] + [ANYWHERE] * len(others),
            )(pieces, *others)
        panels = []
        for kind in self.kinds:
            part = pieces[..., kind.column : kind.column + kind.over * kind.piece]
            part = part.reshape(self.shards, kind.layers, self.sub, kind.over, kind.piece)
            part = part.transpose(3, 1, 2, 0, 4).reshape(kind.over, kind.layers, self.sub, kind.across, self.width)
            panels.append(part.transpose(0, 3, 1, 2, 4).reshape(-1, *self.block_shape[1:]))
        return jnp.concatenate(panels)

    def place(self, fresh, step, one, two):
        shapes = [(kind.layers, kind.rows, kind.cols) for kind in self.kinds]
        if self.aligned:
            before = fresh or []
            return kernel_call(
                functools.partial(place_kernel, self.kinds, self.sub, self.width, step),
                [jax.ShapeDtypeStruct(shape, self.dtype) for shape in shapes],
                2 * self.block_bytes,
                in_specs=[ANYWHERE] * (2 + len(before)),
                out_specs=[ANYWHERE] * len(shapes),
                scratch_shapes=[pltpu.SemaphoreType.DMA],
                input_output_aliases={2 + index: index for index in range(len(before))},
            )(one, two, *before)
        fresh = fresh or [jnp.zeros(shape, self.dtype) for shape in shapes]
        block = jnp.where(at_end(), one, two)
        placed = []
        for kind, target, part in zip(self.kinds, fresh, self.as_kinds(block)):
            part = part.reshape(kind.layers, kind.count, kind.cols)
            placed.append(lax.dynamic_update_slice_in_dim(target, part, block_at(step) * kind.count, 1))
        return placed

    def update(self, moved, weights, momentum, *others):
        if self.aligned:
            units = []
            flat = 0
            for kind in self.kinds:
                for layer in range(kind.layers):
                    for group in range(kind.over):
                        column = kind.column + group * kind.piece
                        units.append((flat, layer * self.sub, self.sub, column, kind.piece))
                        flat = flat + self.sub * self.shards * kind.piece // LANES
            flat_shape = jax.ShapeDtypeStruct((flat, LANES), jnp.float32)
            next_weights, next_momentum, back = kernel_call(
                functools.partial(owner_update_kernel, units, self.shards, self.groups),
                (flat_shape, flat_shape, jax.ShapeDtypeStruct(moved.shape, moved.dtype)),
                10 * self.block_bytes,
                in_specs=[IN_VMEM] * 3 + [ANYWHERE] * len(others),
            )(moved, weights.reshape(flat, LANES), momentum.reshape(flat, LANES), *others)
            return next_weights.reshape(weights.shape), next_momentum.reshape(weights.shape), back
        flats = []
        for kind in self.kinds:
            part = moved[..., kind.column : kind.column + kind.over * kind.piece]
            part = part.reshape(self.shards, kind.layers, self.sub, kind.over, kind.piece)
            flats.append(part.transpose(1, 3, 2, 0, 4).reshape(-1))
        gradient = (wide(jnp.concatenate(flats)) / self.groups).reshape(weights.shape)
        next_momentum = MOMENTUM * momentum + gradient
        next_weights = weights - OUTER_RATE * (gradient + MOMENTUM * next_momentum)
        copies = next_weights.astype(moved.dtype).reshape(-1)
        returning = []
        at = 0
        for kind in self.kinds:
            count = kind.layers * kind.count * kind.cols
            part = copies[at : at + count].reshape(kind.layers, kind.over, self.sub, self.shards, kind.piece)
            returning.append(part.transpose(3, 0, 2, 1, 4).reshape(moved.shape[:2] + (kind.over * kind.piece,)))
            at = at + count
        return next_weights, next_momentum, jnp.concatenate(returning, axis=2)


def local(
    delta_inputs,
    delta_mixing,
    delta_expand,
    delta_reduce,
    owner_weights,
    owner_momentum,
    delta_embed,
    embed_owner,
    embed_momentum,
    basis,
):
    groups = lax.axis_size("rep")
    shards = lax.axis_size("shard")
    side = lax.axis_index("tp")
    end = at_end()
    deltas = (delta_inputs, delta_mixing, delta_expand, delta_reduce)
    dense = Dense(deltas, groups, shards)


    def to_end(value):
        return permute(value, IN_OUT)

    def across(value):
        return permute(value, MIDDLE)

    def to_inner(value):
        return permute(value, OUT_IN)

    rows = embed_owner.shape[2]
    half_rank = basis.shape[1] // 2
    cut = rows // 2 // LANES * LANES
    low, high = narrow_rows(embed_owner, 0, cut), narrow_rows(embed_owner, cut, rows - cut)
    rows_near = [to_end(low), to_end(high)]
    rows_across = [across(low), across(high)]
    rows_far = [to_end(part) for part in rows_across]

    far, middle, near, last = dense.pack(deltas)
    far_in, middle_in, near_in = (to_inner(part) for part in (far, middle, near))
    (far_sum,) = add_after([(far, far_in)], rows_near[0], rows_across[0])
    far_across = across(far_sum)
    middle_sum, last_sum = add_after([(middle, middle_in), (last, far_across)], rows_near[1])
    middle_across = across(middle_sum)
    last_out = to_end(last_sum)
    terms = lax.dot_general(
        after(basis, far),
        wide(delta_embed[0]),
        (((0,), (1,)), ((), ())),
        precision=lax.Precision.HIGH,
        preferred_element_type=jnp.float32,
    ).astype(jnp.bfloat16)
    keep = lax.dynamic_slice_in_dim(terms, side * half_rank, half_rank, 0)
    give = lax.dynamic_slice_in_dim(terms, (1 - side) * half_rank, half_rank, 0)
    (kept,) = add_after([(keep, lax.ppermute(give, "tp", SWAP))], middle_sum)

    def term(place):
        return lax.dynamic_slice_in_dim(kept, block_of(place) * rows, rows, 1)

    terms_out = to_inner(jnp.stack([term(3), term(2), term(1)]))
    rows_inner = [to_inner(low)]
    pieces = dense.split(
        near, last, near_in, middle_across, last_out, rows_far[0], rows_across[1], rows_inner[0]
    )
    rows_inner.append(to_inner(hold(high, pieces)))
    rows_across_2 = [across(part) for part in rows_inner]

    far_terms, middle_terms = add_after([(term(3), terms_out[0]), (term(2), terms_out[1])], pieces)
    terms_middle = across(jnp.stack([far_terms, middle_terms]))

    moved = lax.all_to_all(pieces, "shard", split_axis=0, concat_axis=0, tiled=True)
    rows_across_2[0] = hold(rows_across_2[0], moved)
    rows_last = [to_end(part) for part in rows_across_2]
    next_weights, next_momentum, copies = dense.update(
        moved, owner_weights, owner_momentum, rows_far[1], rows_across_2[0], rows_inner[1]
    )
    (last_terms,) = add_after([(term(0), terms_middle[0])], copies)
    terms_in = to_end(last_terms)
    back = lax.all_to_all(copies, "shard", split_axis=0, concat_axis=0, tiled=True)
    new_block = dense.join(back)
    block_near = permute(new_block, NEAR)
    block_across = across(new_block)

    mine = jnp.where(end, term(0), term(1))
    sent = mean_after(groups, (mine, terms_out[2], terms_middle[1], terms_in), new_block, rows_last[0], rows_across_2[1])
    other = lax.ppermute(sent, "tp", SWAP)

    def both(one, two):
        return jnp.where(side == 0, jnp.concatenate([one, two]), jnp.concatenate([two, one]))

    coefficients = wide(both(sent, other))
    next_embed_momentum = MOMENTUM * embed_momentum[0, 0].T + coefficients
    direction = coefficients + MOMENTUM * next_embed_momentum

    def update(toward, precision):
        return OUTER_RATE * lax.dot_general(
            toward, basis, (((0,), (1,)), ((), ())), precision=precision, preferred_element_type=jnp.float32
        )

    next_embed = embed_owner[0, 0] - update(direction, lax.Precision.HIGH)
    half = lax.dynamic_slice_in_dim(direction, side * half_rank, half_rank, 0).astype(jnp.bfloat16)
    half = after(half, block_near)

    rank = lax.axis_index("rep")
    halves = jnp.stack([permute(half, [(i, (i + step) % groups) for i in range(groups)]) for step in (1, 2, 3)])
    others = lax.ppermute(halves, "tp", SWAP)
    block_far = to_end(block_across)
    block_across_2 = hold(across(block_near), rows_last[1], others)
    block_last = to_end(block_across_2)

    fresh = dense.place(None, 0, new_block, new_block)
    fresh = dense.place(fresh, 1, block_near, block_near)
    fresh = dense.place(fresh, 2, block_far, block_across)
    fresh = dense.place(fresh, 3, block_last, block_across_2)

    fresh_embed = jnp.zeros((groups * rows, embed_owner.shape[3]), jnp.bfloat16)

    def put(target, value, step, start):
        return lax.dynamic_update_slice_in_dim(target, value.astype(target.dtype), block_at(step) * rows + start, 0)

    fresh_embed = put(fresh_embed, next_embed, 0, 0)
    arrived = [(1, rows_near, rows_inner), (2, rows_far, rows_across), (3, rows_last, rows_across_2)]
    for step, at_ends, inside in arrived:
        back_by = (rank - block_at(step) - 1) % groups
        here, there = (lax.dynamic_index_in_dim(part, back_by, 0, False) for part in (halves, others))
        toward = both(here, there)
        for start, one, two in zip((0, cut), at_ends, inside):
            part = jnp.where(end, one, two)
            change = update(wide(toward[:, start : start + part.shape[0]]), lax.Precision.DEFAULT)
            fresh_embed = put(fresh_embed, wide(part) - change, step, start)
    return (
        fresh[0],
        fresh[1],
        fresh[2],
        fresh[3],
        next_weights,
        next_momentum,
        fresh_embed,
        next_embed[None, None],
        next_embed_momentum.T[None, None],
    )


def solution(mesh):
    in_specs = (
        P("rep", None, "shard", "tp"),
        P("rep", None, "shard", "tp"),
        P("rep", None, "shard", "tp"),
        P("rep", None, "shard", "tp"),
        P("rep", "shard", "tp", None),
        P("rep", "shard", "tp", None),
        P("rep", "shard", "tp"),
        P("shard", "rep", None, "tp"),
        P("shard", "rep", None, None),
        P("tp", None),
    )
    out_specs = (
        P(None, "shard", "tp"),
        P(None, "shard", "tp"),
        P(None, "shard", "tp"),
        P(None, "shard", "tp"),
        P("rep", "shard", "tp", None),
        P("rep", "shard", "tp", None),
        P("shard", "tp"),
        P("shard", "rep", None, "tp"),
        P("shard", "rep", None, None),
    )
    return jax.shard_map(local, mesh=mesh, in_specs=in_specs, out_specs=out_specs, check_vma=False)
```
